128 devices in a mesh: ctx: 32 (over y, x, core), fsdp: 4 (over z).
Axes of the slice: x: 4, y: 4, z: 4, core: 2. Of those that a mesh axis runs over, the one named last changes fastest.
Arguments:
- tokens: bfloat16 [4, 4096, 960], P('fsdp', 'ctx'), may hold values from -6 to 6
- cotangent: bfloat16 [4, 4096, 960], P('fsdp', 'ctx'), may hold values from -6 to 6
- slot_blocks: int32 [64], replicated, may hold values from 0 to 63, as said below
- norm_gains: bfloat16 [1920], P('fsdp'), may hold values from 0.5 to 1.5
- w_query: bfloat16 [960, 960], P('fsdp'), may hold values from -0.1875 to 0.1875
- w_key: bfloat16 [960, 320], P('fsdp'), may hold values from -0.1875 to 0.1875
- w_value: bfloat16 [960, 320], P('fsdp'), may hold values from -0.1875 to 0.1875
- w_output: bfloat16 [960, 960], P('fsdp'), may hold values from -3.5 to 3.5
- w_gate: bfloat16 [960, 2560], P('fsdp'), may hold values from -0.1875 to 0.1875
- w_up: bfloat16 [960, 2560], P('fsdp'), may hold values from -0.1875 to 0.1875
- w_down: bfloat16 [2560, 960], P('fsdp'), may hold values from -0.125 to 0.125
Outputs:
- layer_out: bfloat16 [4, 4096, 960], P('fsdp', 'ctx')
- input_grad: float32 [4, 4096, 960], P('fsdp', 'ctx')
- grad_gains: float32 [1920], P(('ctx', 'fsdp'))
- grad_query: float32 [960, 960], P('fsdp', 'ctx')
- grad_key: float32 [960, 320], P('fsdp', 'ctx')
- grad_value: float32 [960, 320], P('fsdp', 'ctx')
- grad_output: float32 [960, 960], P('fsdp', 'ctx')
- grad_gate: float32 [960, 2560], P('fsdp', 'ctx')
- grad_up: float32 [960, 2560], P('fsdp', 'ctx')
- grad_down: float32 [2560, 960], P('fsdp', 'ctx')
The draws below stay inside these ranges and needn't reach their ends.
Inputs may be any that keep to these rules, and one draw needn't show every extreme that they name: `slot_blocks`: A permutation of the 64 blocks of a sequence; entries 2c and 2c + 1 sum to 63.
All inputs are finite; a program needn't handle non-finite values.
Results may differ from the reference program's by a relative error of at most 0.035.
Values may be sent and summed in bfloat16 or wider, within the bound.
A program may use at most 192 MiB of HBM per device.

```python
import math
import jax
import jax.numpy as jnp
from jax import lax

HEADS = 15
KV_HEADS = 5
HEAD_DIM = 64
FF = 2560
BLK = 64
D = 960
KV_DIM = 320
LENGTH = 4096
SEQS = 4
N_CTX = 32


def draw_slot_blocks(key, part):
    key = jax.random.fold_in(key, 7)
    ranking = jax.random.permutation(jax.random.fold_in(key, 1), N_CTX).astype(jnp.int32)
    swapped = jax.random.randint(jax.random.fold_in(key, 2), (N_CTX,), 0, 2).astype(jnp.int32)
    leading = jnp.where(swapped == 1, 2 * N_CTX - 1 - ranking, ranking)
    trailing = 2 * N_CTX - 1 - leading
    return jnp.stack([leading, trailing], axis=1).reshape(2 * N_CTX).astype(jnp.int32)


def level_of(key, dims, cuts, smallest, top_value):
    factor_of = 1.0
    for dim, parts in cuts:
        heights = jax.random.uniform(jax.random.fold_in(jax.random.fold_in(key, 6), dim), (parts,), jnp.float32, smallest / len(cuts), top_value / len(cuts))
        factor_of = factor_of * jnp.repeat(jnp.exp(heights), dims[dim] // parts).reshape((-1,) + (1,) * (len(dims) - 1 - dim))
    return factor_of


def normal_values(key, extent, spread, bound, cuts=(), kind=jnp.bfloat16):
    array = jax.random.normal(key, extent, jnp.float32) * spread
    if len(cuts) > 0:
        array = level_of(key, extent, cuts, -0.22, 0.18) * array
    return jnp.clip(array, min=-bound, max=bound).astype(kind)


def setup_inputs(seed: int = 0) -> dict:
    streams_of = jax.random.split(jax.random.key(seed), 12)
    tokens = normal_values(streams_of[0], (SEQS, LENGTH, D), 1.0, 6.0, ((0, 4), (1, 32)))
    cotangent = normal_values(streams_of[1], (SEQS, LENGTH, D), 1.0, 6.0, ((0, 4), (1, 32)))
    slot_blocks = draw_slot_blocks(jax.random.fold_in(streams_of[11], 71), 0)
    norm_gains = jnp.clip(1.0 + 0.1 * jax.random.normal(streams_of[3], (2 * D,), jnp.float32), 0.5, 1.5).astype(jnp.bfloat16)
    w_query = normal_values(streams_of[4], (D, D), D ** -0.5, 0.1875, ((0, 4),))
    w_key = normal_values(streams_of[5], (D, KV_DIM), D ** -0.5, 0.1875, ((0, 4),))
    w_value = normal_values(streams_of[6], (D, KV_DIM), D ** -0.5, 0.1875, ((0, 4),))
    w_output = normal_values(streams_of[7], (D, D), (max(1, 8 * D // (BLK * N_CTX))) ** -0.5, 3.5, ((0, 4),))
    w_gate = normal_values(streams_of[8], (D, FF), D ** -0.5, 0.1875, ((0, 4),))
    w_up = normal_values(streams_of[9], (D, FF), D ** -0.5, 0.1875, ((0, 4),))
    w_down = normal_values(streams_of[10], (FF, D), FF ** -0.5, 0.125, ((0, 4),))
    return {"tokens": tokens, "cotangent": cotangent, "slot_blocks": slot_blocks, "norm_gains": norm_gains, "w_query": w_query, "w_key": w_key, "w_value": w_value, "w_output": w_output, "w_gate": w_gate, "w_up": w_up, "w_down": w_down}


@jax.custom_vjp
def low(v):
    return lax.optimization_barrier(v.astype(jnp.bfloat16)).astype(jnp.float32)

@jax.custom_vjp
def low_back(v):
    return v

def low_keep(v):
    return (low(v), None)

def low_pass(kept, grad):
    return (grad,)

def back_keep(v):
    return (v, None)

def back_low(kept, grad):
    return (low(grad),)
low.defvjp(low_keep, low_pass)
low_back.defvjp(back_keep, back_low)
epsilon = 1e-05
highest = lax.Precision.HIGHEST

def product(left, right):
    return jnp.dot(left, right, precision=highest)

def rope_tables(positions):
    counter = jnp.arange(HEAD_DIM // 2, dtype=jnp.float32)
    frequency = jnp.exp(counter * (-2.0 * math.log(10000.0) / HEAD_DIM))
    angles = positions.astype(jnp.float32)[:, None] * frequency[None, :]
    return (jnp.cos(angles), jnp.sin(angles))

def rotate(values, cosine, sine):
    half_dim = values.shape[-1] // 2
    first_half = values[..., :half_dim]
    second_half = values[..., half_dim:]
    cos_rows = cosine[:, None, :]
    sin_rows = sine[:, None, :]
    return jnp.concatenate([first_half * cos_rows - second_half * sin_rows, second_half * cos_rows + first_half * sin_rows], axis=-1)

def rms_scale(values, gain):
    return values * lax.rsqrt(lax.optimization_barrier(jnp.mean(values * values, axis=-1, keepdims=True)) + epsilon) * gain

def attend_block(query_block, query_pos, keys, values, key_pos):
    row_count = query_block.shape[0]
    group_size = HEADS // KV_HEADS
    grouped = query_block.reshape(row_count, KV_HEADS, group_size, HEAD_DIM)
    scores = jnp.einsum('bkgd,lkd->kgbl', grouped, keys, precision=highest) * (1.0 / math.sqrt(HEAD_DIM))
    scores = low_back(scores)
    visible = key_pos[None, None, None, :] <= query_pos[None, None, :, None]
    scores = jnp.where(visible, scores, -1e+30)
    row_max = lax.optimization_barrier(jnp.max(scores, axis=-1, keepdims=True))
    exponent = jnp.exp(scores - row_max)
    attn_probs = low(exponent / lax.optimization_barrier(jnp.sum(exponent, axis=-1, keepdims=True)))
    mixed = jnp.einsum('kgbl,lkd->bkgd', attn_probs, values, precision=highest)
    return mixed.reshape(row_count, HEADS * HEAD_DIM)

def layer_sequence(inputs, positions, gains, w_query, w_key, w_value, w_output, w_gate, w_up, w_down):
    length = inputs.shape[0]
    cosine, sine = rope_tables(positions)
    normed_first = low(rms_scale(inputs, gains[:D]))
    query_raw = low_back(product(normed_first, w_query)).reshape(length, HEADS, HEAD_DIM)
    key_raw = low_back(product(normed_first, w_key)).reshape(length, KV_HEADS, HEAD_DIM)
    value_low = low(low_back(product(normed_first, w_value))).reshape(length, KV_HEADS, HEAD_DIM)
    queries = low(rotate(query_raw, cosine, sine))
    keys = low(rotate(key_raw, cosine, sine))
    block_rows = min(512, length)
    blocks = length // block_rows
    attend = jax.checkpoint(attend_block)

    def one_block(pieces):
        return attend(pieces[0], pieces[1], keys, value_low, positions)
    attended = lax.map(one_block, (queries.reshape(blocks, block_rows, HEADS, HEAD_DIM), positions.reshape(blocks, block_rows)))
    attended = low(low_back(attended.reshape(length, D)))
    middle = inputs + low_back(product(attended, w_output))
    normed_second = low(rms_scale(middle, gains[D:]))
    gate_proj = low_back(product(normed_second, w_gate))
    up_proj = low_back(product(normed_second, w_up))
    hidden = low(gate_proj * jax.nn.sigmoid(gate_proj) * up_proj)
    return middle + low_back(product(hidden, w_down))

def reference(tokens, cotangent, slot_blocks, norm_gains, w_query, w_key, w_value, w_output, w_gate, w_up, w_down):
    offsets = jnp.arange(BLK, dtype=jnp.int32)
    positions = (slot_blocks.astype(jnp.int32)[:, None] * BLK + offsets[None, :]).reshape(-1).astype(jnp.int32)
    params = tuple((weight.astype(jnp.float32) for weight in (norm_gains, w_query, w_key, w_value, w_output, w_gate, w_up, w_down)))

    def whole(inputs, *weights):

        def one_sequence(sequence):
            return layer_sequence(sequence, positions, *weights)
        return lax.map(one_sequence, inputs)
    layer_out, pullback = jax.vjp(whole, tokens.astype(jnp.float32), *params)
    grads = pullback(cotangent.astype(jnp.float32))
    return (layer_out.astype(jnp.bfloat16), grads[0], grads[1], grads[2], grads[3], grads[4], grads[5], grads[6], grads[7], grads[8])
```

```python
import math

import jax
import jax.numpy as jnp
from jax import lax
from jax.experimental import pallas as pl
from jax.experimental.pallas import tpu as pltpu
from jax.sharding import Mesh
from jax.sharding import PartitionSpec as P

HEADS = 15
KV_HEADS = 5
HEAD_DIM = 64
GROUP = HEADS // KV_HEADS
BLK = 64
TILE = 512
PAIR = 2 * HEAD_DIM
LANES = 256
D = 960
FF = 2560
CTX = ("y", "x", "c")
ALL = ("y", "x", "c", "z")
TEAM = ("x", "c")

epsilon = 1e-05
NT = (((1,), (1,)), ((), ()))


def multiply(left, right):
    return jnp.dot(left, right, preferred_element_type=jnp.float32)


def multiply_transposed(left, right):
    return lax.dot_general(left, right, NT, preferred_element_type=jnp.float32)


def contract_rows(left, right):
    return lax.dot_general(
        left, right, (((0,), (0,)), ((), ())), preferred_element_type=jnp.float32
    )


def rope_tables(positions):
    counter = jnp.arange(HEAD_DIM // 2, dtype=jnp.float32)
    frequency = jnp.exp(counter * (-2.0 * math.log(10000.0) / HEAD_DIM))
    angles = positions.astype(jnp.float32)[:, None] * frequency[None, :]
    return (jnp.cos(angles), jnp.sin(angles))


def rotate(values, cosine, sine):
    half = HEAD_DIM // 2
    first, second = values[..., :half], values[..., half:]
    cos_rows, sin_rows = cosine[:, None, :], sine[:, None, :]
    return jnp.concatenate(
        [first * cos_rows - second * sin_rows, second * cos_rows + first * sin_rows], axis=-1
    )


def norm_backward(grad_normed, values, inverse_root, gain):
    gain_grad = jnp.sum(grad_normed * values * inverse_root, axis=0)
    scaled = grad_normed * gain
    value_grad = inverse_root * scaled - values * inverse_root**3 * jnp.mean(
        scaled * values, axis=-1, keepdims=True
    )
    return (value_grad, gain_grad)


def load_by_position(slots_ref, kv_hbm, kv, sem):
    def start(slot, _):
        pltpu.make_async_copy(
            kv_hbm.at[slot], kv.at[pl.ds(slots_ref[slot] * BLK, BLK)], sem
        ).start()
        return 0

    lax.fori_loop(0, 64, start, 0)

    pltpu.make_async_copy(kv, kv, sem).wait()


def pick(offset):
    row = lax.broadcasted_iota(jnp.int32, (HEAD_DIM, PAIR), 0)
    lane = lax.broadcasted_iota(jnp.int32, (HEAD_DIM, PAIR), 1)
    return jnp.where(lane == row + offset, 1.0, 0.0).astype(jnp.bfloat16)


def hidden_keys(block):
    key = lax.broadcasted_iota(jnp.int32, (TILE, LANES), 0)
    lane = lax.broadcasted_iota(jnp.int32, (TILE, LANES), 1)
    return key > lax.rem(lane, BLK) + lax.rem(block, TILE // BLK) * BLK


def forward_kernel(slots_ref, mine_ref, q_ref, kv_hbm, out_ref, lse_ref, kv, acc, top, total, sem):
    load_by_position(slots_ref, kv_hbm, kv, sem)
    value_rows = pick(HEAD_DIM)
    for half in range(2):
        block = mine_ref[half]
        full = lax.div(block, TILE // BLK)
        top[...] = jnp.full_like(top, -1e30)
        total[...] = jnp.zeros_like(total)
        acc[...] = jnp.zeros_like(acc)

        def tile(index, masked):
            rows = pl.ds(pl.multiple_of(index * TILE, TILE), TILE)
            hide = hidden_keys(block) if masked else None
            for g in range(KV_HEADS):
                pair = kv[rows, g * PAIR : (g + 1) * PAIR]
                scores = multiply_transposed(pair, q_ref[half, g])
                if masked:
                    scores = jnp.where(hide, -1e30, scores)
                before = top[g]
                now = jnp.maximum(before, jnp.max(scores, axis=0, keepdims=True))
                weights = jnp.exp(scores - now)
                shrink = jnp.exp(before - now)
                top[g] = now
                total[g] = total[g] * shrink + jnp.sum(weights, axis=0, keepdims=True)
                turned = multiply_transposed(value_rows, pair).astype(jnp.bfloat16)
                acc[g] = acc[g] * shrink + multiply(turned, weights.astype(jnp.bfloat16))

        def step(index, _):
            tile(index, False)
            return 0

        lax.fori_loop(0, full, step, 0)
        tile(full, True)
        for g in range(KV_HEADS):
            out_ref[half, g] = acc[g] / total[g]
            lse_ref[half, g] = top[g] + jnp.log(total[g])


def backward_kernel(
    slots_ref, mine_ref, q_ref, do_ref, out_ref, lse_ref, kv_hbm, dq_ref, dkv_hbm,
    kv, grads, low, delta, acc, sem, out_sem,
):
    load_by_position(slots_ref, kv_hbm, kv, sem)
    grads[...] = jnp.zeros_like(grads)
    key_rows = pick(0)
    value_rows = pick(HEAD_DIM)
    for half in range(2):
        block = mine_ref[half]
        full = lax.div(block, TILE // BLK)
        acc[...] = jnp.zeros_like(acc)
        for g in range(KV_HEADS):
            delta[g] = jnp.sum(
                multiply_transposed(value_rows, do_ref[half, g]) * out_ref[half, g],
                axis=0,
                keepdims=True,
            )

        def tile(index, masked):
            rows = pl.ds(pl.multiple_of(index * TILE, TILE), TILE)
            hide = hidden_keys(block) if masked else None
            for g in range(KV_HEADS):
                pair = kv[rows, g * PAIR : (g + 1) * PAIR]
                scores = multiply_transposed(pair, q_ref[half, g])
                weights = jnp.exp(scores - lse_ref[half, g])
                if masked:
                    weights = jnp.where(hide, 0.0, weights)
                grad_weights = multiply_transposed(pair, do_ref[half, g])
                grad_scores = (weights * (grad_weights - delta[g])).astype(jnp.bfloat16)
                grads[rows, g * PAIR : (g + 1) * PAIR] += multiply(
                    grad_scores, q_ref[half, g]
                ) + multiply(weights.astype(jnp.bfloat16), do_ref[half, g])
                turned = multiply_transposed(key_rows, pair).astype(jnp.bfloat16)
                acc[g] += multiply(turned, grad_scores)

        def step(index, _):
            tile(index, False)
            return 0

        lax.fori_loop(0, full, step, 0)
        tile(full, True)
        dq_ref[half] = acc[...] * 0.125

    def lower(index, _):
        rows = pl.ds(pl.multiple_of(index * TILE, TILE), TILE)
        low[rows, :] = grads[rows, :].astype(jnp.bfloat16)
        return 0

    lax.fori_loop(0, low.shape[0] // TILE, lower, 0)

    def start(slot, _):
        ctx = lax.div(slot, 2)
        y, x, c = lax.div(ctx, 8), lax.rem(lax.div(ctx, 2), 4), lax.rem(ctx, 2)
        place = dkv_hbm.at[c, x * (1 - c) + y * c, y * (1 - c) + x * c]
        pltpu.make_async_copy(
            low.at[pl.ds(slots_ref[slot] * BLK, BLK)],
            place.at[pl.ds(lax.rem(slot, 2) * BLK, BLK)],
            out_sem,
        ).start()
        return 0

    lax.fori_loop(0, 64, start, 0)

    pltpu.make_async_copy(low, low, out_sem).wait()


def attend_forward(slots, mine, queries, gathered):
    smem = pl.BlockSpec(memory_space=pltpu.SMEM)
    vmem = pl.BlockSpec(memory_space=pltpu.VMEM)
    length, width = gathered.shape[0] * BLK, gathered.shape[2]
    return pl.pallas_call(
        forward_kernel,
        out_shape=(
            jax.ShapeDtypeStruct((2, KV_HEADS, HEAD_DIM, LANES), jnp.float32),
            jax.ShapeDtypeStruct((2, KV_HEADS, 1, LANES), jnp.float32),
        ),
        in_specs=[smem, smem, vmem, pl.BlockSpec(memory_space=pl.ANY)],
        out_specs=(vmem, vmem),
        scratch_shapes=[
            pltpu.VMEM((length, width), jnp.bfloat16),
            pltpu.VMEM((KV_HEADS, HEAD_DIM, LANES), jnp.float32),
            pltpu.VMEM((KV_HEADS, 1, LANES), jnp.float32),
            pltpu.VMEM((KV_HEADS, 1, LANES), jnp.float32),
            pltpu.SemaphoreType.DMA,
        ],
        compiler_params=pltpu.CompilerParams(vmem_limit_bytes=48 * 2**20),
        cost_estimate=pl.CostEstimate(
            flops=10_000_000_000, bytes_accessed=8_000_000, transcendentals=5_000_000
        ),
    )(slots, mine, queries, gathered)


def attend_backward(slots, mine, queries, grad_out, out, lse, gathered):
    smem = pl.BlockSpec(memory_space=pltpu.SMEM)
    vmem = pl.BlockSpec(memory_space=pltpu.VMEM)
    hbm = pl.BlockSpec(memory_space=pl.ANY)
    length, width = gathered.shape[0] * BLK, gathered.shape[2]
    return pl.pallas_call(
        backward_kernel,
        out_shape=(
            jax.ShapeDtypeStruct((2, KV_HEADS, HEAD_DIM, LANES), jnp.float32),
            jax.ShapeDtypeStruct((2, 4, 4, 2 * BLK, width), jnp.bfloat16),
        ),
        in_specs=[smem, smem, vmem, vmem, vmem, vmem, hbm],
        out_specs=(vmem, hbm),
        scratch_shapes=[
            pltpu.VMEM((length, width), jnp.bfloat16),
            pltpu.VMEM((length, width), jnp.float32),
            pltpu.VMEM((length, width), jnp.bfloat16),
            pltpu.VMEM((KV_HEADS, 1, LANES), jnp.float32),
            pltpu.VMEM((KV_HEADS, HEAD_DIM, LANES), jnp.float32),
            pltpu.SemaphoreType.DMA,
            pltpu.SemaphoreType.DMA,
        ],
        compiler_params=pltpu.CompilerParams(vmem_limit_bytes=48 * 2**20),
        cost_estimate=pl.CostEstimate(
            flops=20_000_000_000, bytes_accessed=12_000_000, transcendentals=5_000_000
        ),
    )(slots, mine, queries, grad_out, out, lse, gathered)


def by_group(values, before):
    parts = values.reshape(2, BLK, KV_HEADS, GROUP, HEAD_DIM).transpose(0, 2, 3, 1, 4)
    parts = parts.reshape(2, KV_HEADS, GROUP * BLK, HEAD_DIM).astype(jnp.bfloat16)
    return jnp.pad(
        parts,
        ((0, 0), (0, 0), (0, LANES - GROUP * BLK), (before, PAIR - HEAD_DIM - before)),
    )


def from_group(turned):
    parts = turned[..., : GROUP * BLK].reshape(2, KV_HEADS, HEAD_DIM, GROUP, BLK)
    return parts.transpose(0, 4, 1, 3, 2).reshape(2 * BLK, HEADS, HEAD_DIM)


MESH_IDS = pl.DeviceIdType.MESH


def remote(source, target, send_sem, recv_sem, device):
    return pltpu.make_async_remote_copy(
        src_ref=source,
        dst_ref=target,
        send_sem=send_sem,
        recv_sem=recv_sem,
        device_id=device,
        device_id_type=MESH_IDS,
    )


def greet(devices):
    barrier = pltpu.get_barrier_semaphore()
    for device in devices:
        pl.semaphore_signal(barrier, inc=1, device_id=device, device_id_type=MESH_IDS)
    pl.semaphore_wait(barrier, len(devices))


def ffn_kernel(
    h_ref, cot_ref, gate_up_ref, down_ref,
    dh_ref, partial_ref, grads_ref,
    rows, grad, hid, dgate, dup, mine, from_sibling, kept, halves, passed, arrived,
    gather_send, gather_recv, sib_send, sib_recv, ring_send, ring_recv,
):
    x, c = lax.axis_index("x"), lax.axis_index("c")
    right, left, across = lax.rem(x + 1, 4), lax.rem(x + 3, 4), lax.rem(x + 2, 4)
    other = 1 - c
    to_right, to_left, to_sibling = {"x": right}, {"x": left}, {"c": other}
    half = BLK
    top, low = pl.ds(0, half), pl.ds(half, half)
    greet((to_right, to_left, to_sibling))

    rows[x, c] = h_ref[...]
    spot = rows.at[x, c]
    first = [
        remote(spot, spot, gather_send.at[0], gather_recv.at[0], to_right),
        remote(spot, spot, gather_send.at[1], gather_recv.at[1], to_left),
        remote(spot, spot, sib_send.at[0], sib_recv.at[0], to_sibling),
    ]
    for copy in first:
        copy.start()
    from_left, from_right, from_far = rows.at[left, c], rows.at[right, c], rows.at[across, c]
    gate_w, up_w = gate_up_ref[0], gate_up_ref[1]
    down_w = down_ref[...]

    def work(chip, step):
        block = rows[chip].reshape(4 * BLK, D)
        gate = multiply(block, gate_w)
        up = multiply(block, up_w)
        grad_hidden = multiply_transposed(cot_ref[chip].reshape(4 * BLK, D), down_w)
        sigmoid = 1.0 / (1.0 + jnp.exp(-gate))
        silu = gate * sigmoid
        hidden = (silu * up).astype(jnp.bfloat16)
        grad_gate = (grad_hidden * up * sigmoid * (1.0 + gate * (1.0 - sigmoid))).astype(jnp.bfloat16)
        grad_up = (grad_hidden * silu).astype(jnp.bfloat16)
        hid[chip] = hidden
        dgate[chip] = grad_gate
        dup[chip] = grad_up
        grad_rows = multiply_transposed(grad_gate, gate_w) + multiply_transposed(grad_up, up_w)
        kept[step] = grad_rows.reshape(2, 2 * BLK, D)
        mine[step] = kept[step, other].astype(jnp.bfloat16)
        copy = remote(
            mine.at[step], from_sibling.at[step], sib_send.at[4 + step], sib_recv.at[4 + step], to_sibling
        )
        copy.start()
        partial_ref[chip] = multiply(hidden, down_w).astype(jnp.bfloat16).reshape(2, 2 * BLK, D)
        return copy

    first[2].wait_recv()
    backs = [work(x, 0)]
    first[0].wait_recv()
    forward_right = remote(
        from_left.at[top], from_left.at[top], gather_send.at[2], gather_recv.at[2], to_right
    )
    forward_right.start()
    sib_left = remote(from_left, from_left, sib_send.at[1], sib_recv.at[1], to_sibling)
    sib_left.start()
    first[1].wait_recv()
    forward_left = remote(
        from_right.at[low], from_right.at[low], gather_send.at[3], gather_recv.at[3], to_left
    )
    forward_left.start()
    sib_right = remote(from_right, from_right, sib_send.at[2], sib_recv.at[2], to_sibling)
    sib_right.start()
    sib_left.wait_recv()
    backs.append(work(left, 1))
    sib_right.wait_recv()
    backs.append(work(right, 2))
    forward_right.wait_recv()
    forward_left.wait_recv()
    sib_far = remote(from_far, from_far, sib_send.at[3], sib_recv.at[3], to_sibling)
    sib_far.start()
    sib_far.wait_recv()
    backs.append(work(across, 3))

    backs[3].wait_recv()
    far = kept[3, c] + from_sibling[3].astype(jnp.float32)
    halves[...] = far.astype(jnp.bfloat16)
    far_right = remote(halves.at[top], arrived.at[0, top], ring_send.at[0], ring_recv.at[0], to_right)
    far_left = remote(halves.at[low], arrived.at[0, low], ring_send.at[1], ring_recv.at[1], to_left)
    far_right.start()
    far_left.start()
    unit = FF // 32
    slabs = [(z, y) for z in range(4) for y in range(4)]

    def keep(start, down):
        for z, y in slabs:
            line, column = (z, y) if down else (y, z)
            piece = grad[
                line * unit : (line + 1) * unit, column * (D // 4) : (column + 1) * (D // 4)
            ]
            grads_ref[z, y, start : start + unit] = piece.astype(jnp.bfloat16)

    grad[...] = contract_rows(
        dgate[...].reshape(16 * BLK, FF // 8), rows[...].reshape(16 * BLK, D)
    )
    keep(0, False)
    for step in range(3):
        backs[step].wait_recv()
        kept[step, c] += from_sibling[step].astype(jnp.float32)
    far_right.wait_recv()
    passed[0, top] = (kept[2, c, top] + arrived[0, top].astype(jnp.float32)).astype(jnp.bfloat16)
    passed[0, low] = kept[2, c, low].astype(jnp.bfloat16)
    near_right = remote(passed.at[0], arrived.at[1], ring_send.at[2], ring_recv.at[2], to_right)
    near_right.start()
    far_left.wait_recv()
    passed[1, top] = kept[1, c, top].astype(jnp.bfloat16)
    passed[1, low] = (kept[1, c, low] + arrived[0, low].astype(jnp.float32)).astype(jnp.bfloat16)
    near_left = remote(passed.at[1], arrived.at[2], ring_send.at[3], ring_recv.at[3], to_left)
    near_left.start()
    grad[...] = contract_rows(
        dup[...].reshape(16 * BLK, FF // 8), rows[...].reshape(16 * BLK, D)
    )
    keep(unit, False)
    grad[...] = contract_rows(
        hid[...].reshape(16 * BLK, FF // 8), cot_ref[...].reshape(16 * BLK, D)
    )
    keep(2 * unit, True)
    near_right.wait_recv()
    near_left.wait_recv()
    dh_ref[...] = (
        kept[0, c] + arrived[1].astype(jnp.float32) + arrived[2].astype(jnp.float32)
    )
    for copy in first + [forward_right, forward_left, sib_left, sib_right, sib_far]:
        copy.wait_send()
    for copy in backs + [far_right, far_left, near_right, near_left]:
        copy.wait_send()


def feed_forward(normed, team_cotangent, gate_up, down):
    vmem = pl.BlockSpec(memory_space=pltpu.VMEM)
    width = FF // 8
    return pl.pallas_call(
        ffn_kernel,
        out_shape=(
            jax.ShapeDtypeStruct((2 * BLK, D), jnp.float32),
            jax.ShapeDtypeStruct((4, 2, 2 * BLK, D), jnp.bfloat16),
            jax.ShapeDtypeStruct((4, 4, 3 * FF // 32, D // 4), jnp.bfloat16),
        ),
        in_specs=[vmem] * 4,
        out_specs=(vmem,) * 3,
        scratch_shapes=[
            pltpu.VMEM((4, 2, 2 * BLK, D), jnp.bfloat16),
            pltpu.VMEM((width, D), jnp.float32),
            pltpu.VMEM((4, 4 * BLK, width), jnp.bfloat16),
            pltpu.VMEM((4, 4 * BLK, width), jnp.bfloat16),
            pltpu.VMEM((4, 4 * BLK, width), jnp.bfloat16),
            pltpu.VMEM((4, 2 * BLK, D), jnp.bfloat16),
            pltpu.VMEM((4, 2 * BLK, D), jnp.bfloat16),
            pltpu.VMEM((4, 2, 2 * BLK, D), jnp.float32),
            pltpu.VMEM((2 * BLK, D), jnp.bfloat16),
            pltpu.VMEM((2, 2 * BLK, D), jnp.bfloat16),
            pltpu.VMEM((3, 2 * BLK, D), jnp.bfloat16),
            pltpu.SemaphoreType.DMA((4,)),
            pltpu.SemaphoreType.DMA((4,)),
            pltpu.SemaphoreType.DMA((8,)),
            pltpu.SemaphoreType.DMA((8,)),
            pltpu.SemaphoreType.DMA((4,)),
            pltpu.SemaphoreType.DMA((4,)),
        ],
        compiler_params=pltpu.CompilerParams(
            collective_id=1, has_side_effects=True, vmem_limit_bytes=56 * 2**20
        ),
        cost_estimate=pl.CostEstimate(
            flops=6_000_000_000, bytes_accessed=12_000_000, transcendentals=400_000
        ),
    )(normed, team_cotangent, gate_up, down)


def ring_of(axis):
    place = lax.axis_index(axis)
    return place, {axis: lax.rem(place + 1, 4)}, {axis: lax.rem(place + 3, 4)}


def plane_rings():
    x, y, c = lax.axis_index("x"), lax.axis_index("y"), lax.axis_index("c")

    def along(step_x, step_y):
        return {"y": lax.rem(y + step_y, 4), "x": lax.rem(x + step_x, 4)}

    first = (x * (1 - c) + y * c, along(1 - c, c), along(3 * (1 - c), 3 * c))
    second = (y * (1 - c) + x * c, along(c, 1 - c), along(3 * c, 3 * (1 - c)))
    return first, second


def cut(rows):
    top = (rows // 2 + 15) // 16 * 16
    return pl.ds(0, top), pl.ds(top, rows - top)


class RingGather:
    def __init__(self, ring, own, spot, parts, send, recv):
        self.place, self.right, self.left = ring
        self.own, self.spot, self.parts, self.send, self.recv = own, spot, parts, send, recv
        self.begun = []

    def _go(self, source, target, index, device):
        copy = remote(source, target, self.send.at[index], self.recv.at[index], device)
        copy.start()
        self.begun.append(copy)
        return copy

    def near(self):
        target = self.spot(self.place)
        self.to_right = self._go(self.own, target, 0, self.right)
        self.to_left = self._go(self.own, target, 1, self.left)

    def from_left(self):
        self.to_right.wait_recv()
        block = self.spot(lax.rem(self.place + 3, 4))
        piece = block.at[self.parts[0]]
        self.on_right = self._go(piece, piece, 2, self.right)
        return block

    def from_right(self):
        self.to_left.wait_recv()
        block = self.spot(lax.rem(self.place + 1, 4))
        piece = block.at[self.parts[1]]
        self.on_left = self._go(piece, piece, 3, self.left)
        return block

    def from_far(self):
        self.on_right.wait_recv()
        self.on_left.wait_recv()
        return self.spot(lax.rem(self.place + 2, 4))

    def drain(self):
        for copy in self.begun:
            copy.wait_send()


class Passing:
    def __init__(self, send, recv):
        self.send, self.recv, self.copies = send, recv, []
        self.device = {"c": 1 - lax.axis_index("c")}

    def go(self, source, target):
        k = len(self.copies)
        copy = remote(source, target, self.send.at[k], self.recv.at[k], self.device)
        copy.start()
        self.copies.append(copy)

    def wait(self):
        for copy in self.copies:
            copy.wait_recv()

    def drain(self):
        for copy in self.copies:
            copy.wait_send()


def first_gather_kernel(
    w_ref, gain_ref, w_out, gain_out,
    w_send, w_recv, gain_send, gain_recv, sib_send, sib_recv, local,
):
    c = lax.axis_index("c")
    z_ring = ring_of("z")
    greet((z_ring[1], z_ring[2], {"c": 1 - c}))
    passing = Passing(sib_send, sib_recv)
    weights = RingGather(
        z_ring, w_ref.at[c], lambda i: w_out.at[c, i], cut(w_ref.shape[1]), w_send, w_recv
    )
    gains = RingGather(
        z_ring, gain_ref, lambda i: gain_out.at[i], cut(gain_ref.shape[0]), gain_send, gain_recv
    )
    weights.near()
    gains.near()
    z = z_ring[0]
    own = [
        pltpu.make_async_copy(w_ref, w_out.at[:, z], local.at[0]),
        pltpu.make_async_copy(gain_ref, gain_out.at[z], local.at[1]),
    ]
    for copy in own:
        copy.start()
    for turn in ("from_left", "from_right", "from_far"):
        block = getattr(weights, turn)()
        passing.go(block, block)
        getattr(gains, turn)()
    passing.wait()
    for copy in own:
        copy.wait()
    weights.drain()
    gains.drain()
    passing.drain()


def second_gather_kernel(
    kv_ref, o_ref, down_ref, kv_out, o_out, down_out,
    kv_send, kv_recv, o_send, o_recv, down_send, down_recv, sib_send, sib_recv, o_sib_send, o_sib_recv, local,
):
    x, y, c = lax.axis_index("x"), lax.axis_index("y"), lax.axis_index("c")
    z_ring = ring_of("z")
    first, second = plane_rings()
    greet((first[1], first[2], second[1], second[2], z_ring[1], z_ring[2], {"c": 1 - c}))
    a0 = first[0]

    def spot(a, b):
        return kv_out.at[b * (1 - c) + a * c, a * (1 - c) + b * c, c]

    rows = cut(kv_ref.shape[0])
    passing = Passing(sib_send, sib_recv)
    o_passing = Passing(o_sib_send, o_sib_recv)

    def hand(block):
        passing.go(block, block)

    stage = RingGather(
        first, kv_ref, lambda a: spot(a, second[0]), rows, kv_send.at[0], kv_recv.at[0]
    )

    def spread_ring(k, shift, own):
        a = lax.rem(a0 + shift, 4)
        ring = RingGather(
            second, own, lambda b: spot(a, b), rows, kv_send.at[1 + k], kv_recv.at[1 + k]
        )
        ring.near()
        return ring

    stage.near()
    ring_own = spread_ring(0, 0, kv_ref)
    passing.go(kv_ref, spot(a0, second[0]))
    z_rings = (
        RingGather(z_ring, o_ref.at[c], lambda i: o_out.at[c, i], cut(o_ref.shape[1]), o_send, o_recv),
        RingGather(z_ring, down_ref, lambda i: down_out.at[i], cut(down_ref.shape[0]), down_send, down_recv),
    )
    for ring in z_rings:
        ring.near()
    z = z_ring[0]
    own = [
        pltpu.make_async_copy(kv_ref, kv_out.at[y, x, c], local.at[0]),
        pltpu.make_async_copy(o_ref, o_out.at[:, z], local.at[1]),
        pltpu.make_async_copy(down_ref, down_out.at[z], local.at[2]),
    ]
    for copy in own:
        copy.start()
    block = stage.from_left()
    ring_left = spread_ring(1, 3, block)
    hand(block)
    block = stage.from_right()
    ring_right = spread_ring(2, 1, block)
    hand(block)
    block = stage.from_far()
    ring_far = spread_ring(3, 2, block)
    hand(block)
    plane = (ring_own, ring_left, ring_right, ring_far)
    for turn in ("from_left", "from_right"):
        for ring in plane:
            hand(getattr(ring, turn)())
        block = getattr(z_rings[0], turn)()
        o_passing.go(block, block)
        getattr(z_rings[1], turn)()
    for ring in plane:
        hand(ring.from_far())
    block = z_rings[0].from_far()
    o_passing.go(block, block)
    z_rings[1].from_far()
    passing.wait()
    o_passing.wait()
    for copy in own:
        copy.wait()
    for ring in (stage,) + plane + z_rings:
        ring.drain()
    passing.drain()
    o_passing.drain()


def dma(*counts):
    return [pltpu.SemaphoreType.DMA(n if isinstance(n, tuple) else (n,)) for n in counts]


def first_gather(weights, gains):
    hbm = pl.BlockSpec(memory_space=pl.ANY)
    return pl.pallas_call(
        first_gather_kernel,
        out_shape=(
            jax.ShapeDtypeStruct((2, 4) + weights.shape[1:], weights.dtype),
            jax.ShapeDtypeStruct((4,) + gains.shape, gains.dtype),
        ),
        in_specs=[hbm] * 2,
        out_specs=(hbm,) * 2,
        scratch_shapes=dma(4, 4, 4, 4, 3, 3, 2),
        compiler_params=pltpu.CompilerParams(collective_id=2, has_side_effects=True),
        cost_estimate=pl.CostEstimate(flops=0, bytes_accessed=60_000_000, transcendentals=0),
    )(weights, gains)


def second_gather(kv, weight, down):
    hbm = pl.BlockSpec(memory_space=pl.ANY)
    return pl.pallas_call(
        second_gather_kernel,
        out_shape=(
            jax.ShapeDtypeStruct((4, 4, 2) + kv.shape, kv.dtype),
            jax.ShapeDtypeStruct((2, 4) + weight.shape[1:], weight.dtype),
            jax.ShapeDtypeStruct((4,) + down.shape, down.dtype),
        ),
        in_specs=[hbm] * 3,
        out_specs=(hbm,) * 3,
        scratch_shapes=dma((5, 4), (5, 4), 4, 4, 4, 4, 16, 16, 3, 3, 3),
        compiler_params=pltpu.CompilerParams(collective_id=3, has_side_effects=True),
        cost_estimate=pl.CostEstimate(flops=0, bytes_accessed=100_000_000, transcendentals=0),
    )(kv, weight, down)


class RingSum:
    def __init__(self, ring, value, parts, far, passed, far_in, near_in, send, recv):
        self.place, self.right, self.left = ring
        self.value, self.parts = value, parts
        self.far, self.passed, self.far_in, self.near_in = far, passed, far_in, near_in
        self.send, self.recv = send, recv
        self.begun = []

    def _go(self, source, target, index, device):
        copy = remote(source, target, self.send.at[index], self.recv.at[index], device)
        copy.start()
        self.begun.append(copy)
        return copy

    def send_far(self):
        top, low = self.parts
        other = lax.rem(self.place + 2, 4)
        for part in self.parts:
            self.far[part] = self.value(other, part).astype(jnp.bfloat16)
        self.far_right = self._go(self.far.at[top], self.far_in.at[top], 0, self.right)
        self.far_left = self._go(self.far.at[low], self.far_in.at[low], 1, self.left)

    def send_right(self):
        top, low = self.parts
        other = lax.rem(self.place + 1, 4)
        self.passed[0, low] = self.value(other, low).astype(jnp.bfloat16)
        self.far_right.wait_recv()
        total = self.value(other, top) + self.far_in[top].astype(jnp.float32)
        self.passed[0, top] = total.astype(jnp.bfloat16)
        self.near_right = self._go(self.passed.at[0], self.near_in.at[0], 2, self.right)

    def send_left(self):
        top, low = self.parts
        other = lax.rem(self.place + 3, 4)
        self.passed[1, top] = self.value(other, top).astype(jnp.bfloat16)
        self.far_left.wait_recv()
        total = self.value(other, low) + self.far_in[low].astype(jnp.float32)
        self.passed[1, low] = total.astype(jnp.bfloat16)
        self.near_left = self._go(self.passed.at[1], self.near_in.at[1], 3, self.left)

    def arrive(self):
        self.near_right.wait_recv()
        self.near_left.wait_recv()

    def total(self, part):
        return (
            self.value(self.place, part)
            + self.near_in[0, part].astype(jnp.float32)
            + self.near_in[1, part].astype(jnp.float32)
        )

    def drain(self):
        for copy in self.begun:
            copy.wait_send()


def ring_scratch(shape):
    return [
        pltpu.VMEM(shape, jnp.bfloat16),
        pltpu.VMEM((2,) + shape, jnp.bfloat16),
        pltpu.VMEM(shape, jnp.bfloat16),
        pltpu.VMEM((2,) + shape, jnp.bfloat16),
        pltpu.SemaphoreType.DMA((4,)),
        pltpu.SemaphoreType.DMA((4,)),
    ]


HALVES = (pl.ds(0, 2), pl.ds(2, 2))


class PlaneSum:
    def __init__(self, rings, parts, theirs, one, two, sib_send, sib_recv):
        self.first, self.second = rings
        self.parts, self.theirs = parts, theirs
        self.c = lax.axis_index("c")
        self.sib_send, self.sib_recv = sib_send, sib_recv
        middle, one, two = one[0], one[1:], two
        self.middle = middle
        shape = middle.shape[1:]
        self.rows = (pl.ds(0, shape[0] // 2), pl.ds(shape[0] // 2, shape[0] // 2))
        self.ring_one = RingSum(self.first, self._both, HALVES, *one)
        self.ring_two = RingSum(self.second, self._middle, self.rows, *two)

    def _both(self, a, part):
        mine = self.parts[self.c, a, part].astype(jnp.float32)
        return mine + self.theirs[a, part].astype(jnp.float32)

    def _middle(self, b, part):
        return self.middle[b, part].astype(jnp.float32)

    def hand(self, k):
        a = lax.rem(self.second[0] + (2, 1, 3, 0)[k], 4)
        copy = remote(
            self.parts.at[1 - self.c, a],
            self.theirs.at[a],
            self.sib_send.at[k],
            self.sib_recv.at[k],
            {"c": 1 - self.c},
        )
        copy.start()
        return copy

    def along_first(self, handed):
        one = self.ring_one
        handed[0].wait_recv()
        one.send_far()
        handed[1].wait_recv()
        one.send_right()
        handed[2].wait_recv()
        one.send_left()
        handed[3].wait_recv()

    def along_second(self):
        one, two = self.ring_one, self.ring_two
        one.arrive()
        for part in HALVES:
            self.middle[part] = one.total(part).astype(jnp.bfloat16)
        two.send_far()
        two.send_right()
        two.send_left()

    def drain(self, handed):
        for copy in handed:
            copy.wait_send()
        self.ring_one.drain()
        self.ring_two.drain()


ORDER = (2, 1, 3, 0)


def fill(plane, left_ref, right_ref):
    c = lax.axis_index("c")
    wide = left_ref.shape[3]

    def product(core, a):
        lhs = left_ref[core, a].reshape(4 * wide, left_ref.shape[4])
        for z in range(4):
            block = multiply(lhs, right_ref[z]).astype(jnp.bfloat16)
            plane.parts[core, a, :, z] = block.reshape(4, wide, block.shape[1])

    handed = []
    for k in range(4):
        product(1 - c, lax.rem(plane.second[0] + ORDER[k], 4))
        handed.append(plane.hand(k))
    for k in range(4):
        product(c, lax.rem(plane.first[0] + ORDER[k], 4))
    return handed


def pairs_sum_kernel(
    parts, ffn, left_ref, right_ref, kv_out, ffn_out, out_ref,
    theirs, middle, products, their_products, products_middle, last, *scratch,
):
    sems, rest = scratch[:4], scratch[4:]
    one, two, three, four, five, six = (rest[6 * k : 6 * k + 6] for k in range(6))
    first, second = plane_rings()
    z_ring = ring_of("z")
    greet((first[1], first[2], second[1], second[2], z_ring[1], z_ring[2], {"c": 1 - lax.axis_index("c")}))
    pairs = PlaneSum((first, second), parts, theirs, (middle,) + one, two, *sems[:2])
    weights = PlaneSum(
        (first, second), products, their_products, (products_middle,) + four, five, *sems[2:]
    )
    handed = [pairs.hand(k) for k in range(4)]
    along_z = RingSum(
        z_ring, lambda i, part: ffn[i, part].astype(jnp.float32), HALVES, *three
    )
    along_z.send_far()
    handed_weights = fill(weights, left_ref, right_ref)
    pairs.along_first(handed)
    weights.along_first(handed_weights)
    along_z.send_right()
    along_z.send_left()
    pairs.along_second()
    weights.along_second()
    pairs.ring_two.arrive()
    for part in pairs.rows:
        kv_out[part] = pairs.ring_two.total(part)
    weights.ring_two.arrive()
    for part in weights.rows:
        last[part] = weights.ring_two.total(part)
    weights_z = RingSum(z_ring, lambda i, part: last[i, part], cut(left_ref.shape[3]), *six)
    weights_z.send_far()
    along_z.arrive()
    for part in HALVES:
        ffn_out[part] = along_z.total(part).astype(jnp.bfloat16)
    weights_z.send_right()
    weights_z.send_left()
    weights_z.arrive()
    for part in weights_z.parts:
        out_ref[part] = weights_z.total(part)
    pairs.drain(handed)
    weights.drain(handed_weights)
    along_z.drain()
    weights_z.drain()


def pairs_sum(parts, ffn, left, right):
    vmem = pl.BlockSpec(memory_space=pltpu.VMEM)
    block, share = parts.shape[3:], ffn.shape[2:]
    weight = (left.shape[3], right.shape[2])
    return pl.pallas_call(
        pairs_sum_kernel,
        out_shape=(
            jax.ShapeDtypeStruct(block, jnp.float32),
            jax.ShapeDtypeStruct((4,) + share, jnp.bfloat16),
            jax.ShapeDtypeStruct(weight, jnp.float32),
        ),
        in_specs=[vmem] * 4,
        out_specs=(vmem,) * 3,
        scratch_shapes=[
            pltpu.VMEM((4, 4) + block, jnp.bfloat16),
            pltpu.VMEM((4,) + block, jnp.bfloat16),
            pltpu.VMEM((2, 4, 4, 4) + weight, jnp.bfloat16),
            pltpu.VMEM((4, 4, 4) + weight, jnp.bfloat16),
            pltpu.VMEM((4, 4) + weight, jnp.bfloat16),
            pltpu.VMEM((4,) + weight, jnp.float32),
        ]
        + dma(4, 4, 4, 4)
        + ring_scratch((4,) + block)
        + ring_scratch(block)
        + ring_scratch((4,) + share)
        + ring_scratch((4, 4) + weight)
        + ring_scratch((4,) + weight)
        + ring_scratch(weight),
        compiler_params=pltpu.CompilerParams(
            collective_id=4, has_side_effects=True, vmem_limit_bytes=60 * 2**20
        ),
    )(parts, ffn, left, right)


def weights_sum_kernel(
    left_ref, right_ref, gain_ref, ffn_ref, out_ref, gain_out, ffn_out, down_out,
    parts, theirs, middle, last, gain_in, gain_now, down_own, *scratch,
):
    sems, rest = scratch[:2], scratch[2:]
    one, two, three, four = (rest[6 * k : 6 * k + 6] for k in range(4))
    gain_send, gain_recv, down_send, down_recv, down_sib_send, down_sib_recv, local = rest[24:]
    x, c = lax.axis_index("x"), lax.axis_index("c")
    first, second = plane_rings()
    z_ring, x_ring, y_ring = ring_of("z"), ring_of("x"), ring_of("y")
    far = {"x": {"x": lax.rem(x + 2, 4)}}
    far["y"] = {"y": lax.rem(lax.axis_index("y") + 2, 4)}
    far["z"] = {"z": lax.rem(lax.axis_index("z") + 2, 4)}
    greet(
        (first[1], first[2], second[1], second[2], z_ring[1], z_ring[2], {"c": 1 - c})
        + (far["x"], far["y"], far["z"])
    )
    along_y = RingSum(
        y_ring,
        lambda i, part: ffn_ref[i, part].astype(jnp.float32),
        cut(ffn_ref.shape[1]),
        *four,
    )
    along_y.send_far()
    third = down_own.shape[0]
    downs = RingGather(
        x_ring, down_own, lambda i: down_out.at[i, c], cut(third), down_send, down_recv
    )
    passing = Passing(down_sib_send, down_sib_recv)
    own = pltpu.make_async_copy(down_own, down_out.at[x, c], local)

    plane = PlaneSum((first, second), parts, theirs, (middle,) + one, two, *sems)
    handed = fill(plane, left_ref, right_ref)
    along_y.send_right()
    along_y.send_left()

    sent = []

    def share(index, devices):
        copies = [
            remote(
                gain_now.at[index],
                gain_in.at[index, k],
                gain_send.at[index, k],
                gain_recv.at[index, k],
                device,
            )
            for k, device in enumerate(devices)
        ]
        for copy in copies:
            copy.start()
        return copies

    def collect(index, copies):
        total = gain_now[index]
        for k, copy in enumerate(copies):
            copy.wait_recv()
            total = total + gain_in[index, k]
        sent.extend(copies)
        return total

    gain_now[0] = gain_ref[...]
    step = share(0, ({"c": 1 - c},))

    gain_now[1] = collect(0, step)
    step = share(1, (x_ring[1], x_ring[2], far["x"]))

    plane.along_first(handed)
    along_y.arrive()
    for part in along_y.parts:
        ffn_out[part] = along_y.total(part).astype(jnp.bfloat16)
    down_own[...] = ffn_out[2 * third : 3 * third]
    downs.near()
    passing.go(down_own, down_out.at[x, c])
    own.start()
    plane.along_second()
    plane.ring_two.arrive()
    for turn in ("from_left", "from_right", "from_far"):
        block = getattr(downs, turn)()
        passing.go(block, block)
    gain_now[2] = collect(1, step)
    step = share(2, (y_ring[1], y_ring[2], far["y"]))
    for part in plane.rows:
        last[part] = plane.ring_two.total(part)
    along_z = RingSum(z_ring, lambda i, part: last[i, part], cut(left_ref.shape[3]), *three)
    along_z.send_far()
    along_z.send_right()
    along_z.send_left()
    gain_now[3] = collect(2, step)
    step = share(3, (z_ring[1], z_ring[2], far["z"]))
    along_z.arrive()
    for part in along_z.parts:
        out_ref[part] = along_z.total(part)
    gain_out[...] = collect(3, step)
    passing.wait()
    own.wait()
    plane.drain(handed)
    along_z.drain()
    along_y.drain()
    downs.drain()
    passing.drain()
    for copy in sent:
        copy.wait_send()


def weights_sum(left, right, gains, ffn):
    vmem = pl.BlockSpec(memory_space=pltpu.VMEM)
    hbm = pl.BlockSpec(memory_space=pl.ANY)
    block = (left.shape[3], right.shape[2])
    share = ffn.shape[1:]
    down = (share[0] // 3, share[1])
    return pl.pallas_call(
        weights_sum_kernel,
        out_shape=(
            jax.ShapeDtypeStruct(block, jnp.float32),
            jax.ShapeDtypeStruct(gains.shape, jnp.float32),
            jax.ShapeDtypeStruct(share, jnp.bfloat16),
            jax.ShapeDtypeStruct((4, 2) + down, jnp.bfloat16),
        ),
        in_specs=[vmem] * 4,
        out_specs=(vmem, vmem, vmem, hbm),
        scratch_shapes=[
            pltpu.VMEM((2, 4, 4, 4) + block, jnp.bfloat16),
            pltpu.VMEM((4, 4, 4) + block, jnp.bfloat16),
            pltpu.VMEM((4, 4) + block, jnp.bfloat16),
            pltpu.VMEM((4,) + block, jnp.float32),
            pltpu.VMEM((4, 3) + gains.shape, jnp.float32),
            pltpu.VMEM((4,) + gains.shape, jnp.float32),
            pltpu.VMEM(down, jnp.bfloat16),
        ]
        + dma(4, 4)
        + ring_scratch((4, 4) + block)
        + ring_scratch((4,) + block)
        + ring_scratch(block)
        + ring_scratch(share)
        + dma((4, 3), (4, 3), 4, 4, 4, 4)
        + [pltpu.SemaphoreType.DMA],
        compiler_params=pltpu.CompilerParams(
            collective_id=5, has_side_effects=True, vmem_limit_bytes=60 * 2**20
        ),
    )(left, right, gains, ffn)


def shards(
    tokens, cotangent, slot_blocks, norm_gains,
    w_query, w_key, w_value, w_output, w_gate, w_up, w_down,
):
    inputs = tokens[0].astype(jnp.float32)
    row_count = inputs.shape[0]
    ctx_index = lax.axis_index(CTX)
    member = lax.axis_index(TEAM)
    mine = lax.dynamic_slice_in_dim(slot_blocks, 2 * ctx_index, 2)
    offsets = jnp.arange(BLK, dtype=jnp.int32)
    local_pos = (mine[:, None] * BLK + offsets[None, :]).reshape(row_count)
    cosine, sine = rope_tables(local_pos)

    kv_parts = [
        w[:, h * HEAD_DIM : (h + 1) * HEAD_DIM] for h in range(KV_HEADS) for w in (w_key, w_value)
    ]
    w_kv = jnp.concatenate(kv_parts, axis=1)
    wide = w_kv.shape[1] // 2
    gain_rows = jnp.pad(norm_gains, (0, 32 * 128 - norm_gains.shape[0])).reshape(32, 128)
    full_kv, gains = first_gather(jnp.stack([w_kv[:, :wide], w_kv[:, wide:]]), gain_rows)
    full_kv = full_kv.reshape(2, D, wide)
    gains = gains.reshape(4, -1)[:, : D // 2].reshape(2 * D).astype(jnp.float32)

    source = jnp.arange(FF // 8, dtype=jnp.int32)
    source = source // (FF // 32) * (FF // 4) + member * (FF // 32) + source % (FF // 32)
    picked = (jnp.arange(FF, dtype=jnp.int32)[:, None] == source[None, :]).astype(jnp.bfloat16)
    my_gate_up = jnp.stack(
        [multiply(w_gate, picked).astype(jnp.bfloat16), multiply(w_up, picked).astype(jnp.bfloat16)]
    )
    my_down = lax.dynamic_slice_in_dim(w_down, member * (FF // 32), FF // 32)
    upstream_low = cotangent[0]
    gate_up = lax.all_gather(my_gate_up, "z", axis=1, tiled=True)
    full_output = lax.all_gather(w_output, "z", axis=0, tiled=True)
    team_upstream = lax.all_gather(cotangent, TEAM, axis=0, tiled=True)
    my_query = jnp.stack([w_query[:, : D // 2], w_query[:, D // 2 :]])
    gain_first, gain_second = gains[:D], gains[D:]

    root_first = lax.rsqrt(jnp.mean(inputs * inputs, axis=-1, keepdims=True) + epsilon)
    normed_first = (inputs * root_first * gain_first).astype(jnp.bfloat16)
    raw_kv = jnp.concatenate(
        [multiply(normed_first, full_kv[0]), multiply(normed_first, full_kv[1])], axis=1
    )
    pairs = raw_kv.reshape(row_count, KV_HEADS, 2, HEAD_DIM)
    keys = rotate(pairs[:, :, 0], cosine, sine)
    packed = jnp.stack([keys, pairs[:, :, 1]], axis=2).astype(jnp.bfloat16)
    packed = packed.reshape(row_count, KV_HEADS * PAIR)
    gathered, full_query, down = second_gather(packed, my_query, my_down)
    down = down.reshape(FF // 8, D)
    gathered = gathered.reshape(64, BLK, KV_HEADS * PAIR)
    full_query = full_query.reshape(2, D, D // 2)
    raw = jnp.concatenate(
        [multiply(normed_first, full_query[0]), multiply(normed_first, full_query[1])], axis=1
    )
    queries = rotate(raw.reshape(row_count, HEADS, HEAD_DIM), cosine, sine)
    query_rows = by_group(queries.astype(jnp.bfloat16) * jnp.bfloat16(0.125), 0)
    out_turned, lse = attend_forward(slot_blocks, mine, query_rows, gathered)
    attended = from_group(out_turned).reshape(row_count, D).astype(jnp.bfloat16)
    middle = inputs + multiply(attended, full_output)

    root_second = lax.rsqrt(jnp.mean(middle * middle, axis=-1, keepdims=True) + epsilon)
    normed_second = (middle * root_second * gain_second).astype(jnp.bfloat16)
    grad_normed_second, partial, grad_ffn = feed_forward(
        normed_second, team_upstream.reshape(4, 2, row_count, D), gate_up, down
    )
    down_sum = lax.psum_scatter(
        partial.reshape(8, row_count, D), TEAM, scatter_dimension=0, tiled=True
    )

    norm_part, gain_grad_second = norm_backward(
        grad_normed_second, middle, root_second, gain_second
    )
    grad_middle = upstream_low.astype(jnp.float32) + norm_part
    middle_low = grad_middle.astype(jnp.bfloat16)

    grad_attended = multiply_transposed(middle_low, full_output).astype(jnp.bfloat16)

    grad_rows = by_group(grad_attended.reshape(row_count, HEADS, HEAD_DIM), HEAD_DIM)
    query_turned, grad_pairs = attend_backward(
        slot_blocks, mine, query_rows, grad_rows, out_turned, lse, gathered
    )
    grad_query_raw = rotate(from_group(query_turned), cosine, -sine)
    grad_query_raw = grad_query_raw.reshape(row_count, D).astype(jnp.bfloat16)

    def by_owner(columns):
        columns = columns.reshape((4, 4, 2) + columns.shape[1:])
        return jnp.stack([columns[:, :, 0].swapaxes(0, 1), columns[:, :, 1]])

    above = jnp.pad(grad_query_raw.reshape(row_count, 32, 30), ((0, 0), (0, 0), (0, 34)))
    below = jnp.pad(middle_low.reshape(row_count, 32, 30), ((0, 0), (0, 0), (30, 4)))
    columns = by_owner(jnp.concatenate([above, below], axis=0).transpose(1, 2, 0))
    rows = jnp.concatenate([normed_first, attended], axis=0)
    rows = rows.reshape(2 * row_count, 4, D // 4).swapaxes(0, 1)
    own_pairs, part_ffn, sum_query_output = pairs_sum(grad_pairs, grad_ffn, columns, rows)
    own_pairs = own_pairs.reshape(row_count, KV_HEADS, 2, HEAD_DIM)
    grad_key_raw = rotate(own_pairs[:, :, 0], cosine, -sine)
    grad_kv = jnp.stack([grad_key_raw, own_pairs[:, :, 1]], axis=2)
    grad_kv = grad_kv.reshape(row_count, -1).astype(jnp.bfloat16)
    grad_normed_first = multiply_transposed(grad_query_raw[:, : D // 2], full_query[0])
    grad_normed_first += multiply_transposed(grad_query_raw[:, D // 2 :], full_query[1])
    grad_normed_first += multiply_transposed(grad_kv[:, :wide], full_kv[0])
    grad_normed_first += multiply_transposed(grad_kv[:, wide:], full_kv[1])
    norm_first_part, gain_grad_first = norm_backward(
        grad_normed_first, inputs, root_first, gain_first
    )
    input_grad = grad_middle + norm_first_part

    kv_columns = grad_kv.reshape(row_count, KV_HEADS, 2, HEAD_DIM)
    k_columns = kv_columns[:, :, 0].reshape(row_count, 32, 10)
    v_columns = kv_columns[:, :, 1].reshape(row_count, 32, 10)
    columns = jnp.concatenate([k_columns, v_columns], axis=2)
    columns = jnp.pad(columns, ((0, 0), (0, 0), (0, 12))).transpose(1, 2, 0)
    gain_grads = jnp.pad(
        jnp.concatenate([gain_grad_first, gain_grad_second]), (0, 128)
    ).reshape(16, 128)
    sum_pair, sum_gains, sum_ffn, team_down = weights_sum(
        by_owner(columns), rows[:, :row_count], gain_grads, part_ffn
    )
    down_sum, sum_pair = lax.optimization_barrier((down_sum, sum_pair))
    layer_out = (middle + down_sum[0].astype(jnp.float32)).astype(jnp.bfloat16)[None]
    sum_query_output, sum_pair = sum_query_output.T, sum_pair.T
    ffn_columns = sum_ffn[:160].T.astype(jnp.float32)
    sum_down = lax.dynamic_slice_in_dim(
        team_down.reshape(FF // 4, D // 4), member * 30, 30, axis=1
    ).astype(jnp.float32)
    place = (ctx_index * 4 + lax.axis_index("z")) * 15
    return (
        layer_out,
        input_grad[None],
        lax.dynamic_slice_in_dim(sum_gains.reshape(-1), place, 15),
        sum_query_output[:, :30],
        sum_pair[:, :10],
        sum_pair[:, 10:20],
        sum_query_output[:, 30:60],
        ffn_columns[:, :80],
        ffn_columns[:, 80:],
        sum_down,
    )


def solution(mesh):
    fine = Mesh(mesh.devices.reshape(4, 4, 2, 4), ALL)
    weight = P("z", None)
    return jax.shard_map(
        shards,
        mesh=fine,
        in_specs=(
            P("z", CTX, None),
            P("z", CTX, None),
            P(),
            P("z"),
        )
        + (weight,) * 7,
        out_specs=(
            P("z", CTX, None),
            P("z", CTX, None),
            P(ALL),
        )
        + (P("z", CTX),) * 7,
        check_vma=False,
    )
```

```python
import math

import jax
import jax.numpy as jnp
from jax import lax
from jax.experimental import pallas as pl
from jax.experimental.pallas import tpu as pltpu
from jax.sharding import Mesh
from jax.sharding import PartitionSpec as P

HEADS = 15
KV_HEADS = 5
HEAD_DIM = 64
GROUP = HEADS // KV_HEADS
BLK = 64
TILE = 512
PAIR = 2 * HEAD_DIM
LANES = 256
D = 960
FF = 2560
CTX = ("y", "x", "c")
ALL = ("y", "x", "c", "z")
TEAM = ("x", "c")

epsilon = 1e-05
NT = (((1,), (1,)), ((), ()))


def multiply(left, right):
    return jnp.dot(left, right, preferred_element_type=jnp.float32)


def multiply_transposed(left, right):
    return lax.dot_general(left, right, NT, preferred_element_type=jnp.float32)


def contract_rows(left, right):
    return lax.dot_general(
        left, right, (((0,), (0,)), ((), ())), preferred_element_type=jnp.float32
    )


def rope_tables(positions):
    counter = jnp.arange(HEAD_DIM // 2, dtype=jnp.float32)
    frequency = jnp.exp(counter * (-2.0 * math.log(10000.0) / HEAD_DIM))
    angles = positions.astype(jnp.float32)[:, None] * frequency[None, :]
    return (jnp.cos(angles), jnp.sin(angles))


def rotate(values, cosine, sine):
    half = HEAD_DIM // 2
    first, second = values[..., :half], values[..., half:]
    cos_rows, sin_rows = cosine[:, None, :], sine[:, None, :]
    return jnp.concatenate(
        [first * cos_rows - second * sin_rows, second * cos_rows + first * sin_rows], axis=-1
    )


def norm_backward(grad_normed, values, inverse_root, gain):
    gain_grad = jnp.sum(grad_normed * values * inverse_root, axis=0)
    scaled = grad_normed * gain
    value_grad = inverse_root * scaled - values * inverse_root**3 * jnp.mean(
        scaled * values, axis=-1, keepdims=True
    )
    return (value_grad, gain_grad)


def load_by_position(slots_ref, kv_hbm, kv, sem):
    def start(slot, _):
        pltpu.make_async_copy(
            kv_hbm.at[slot], kv.at[pl.ds(slots_ref[slot] * BLK, BLK)], sem
        ).start()
        return 0

    lax.fori_loop(0, 64, start, 0)

    pltpu.make_async_copy(kv, kv, sem).wait()


def pick(offset):
    row = lax.broadcasted_iota(jnp.int32, (HEAD_DIM, PAIR), 0)
    lane = lax.broadcasted_iota(jnp.int32, (HEAD_DIM, PAIR), 1)
    return jnp.where(lane == row + offset, 1.0, 0.0).astype(jnp.bfloat16)


def hidden_keys(block):
    key = lax.broadcasted_iota(jnp.int32, (TILE, LANES), 0)
    lane = lax.broadcasted_iota(jnp.int32, (TILE, LANES), 1)
    return key > lax.rem(lane, BLK) + lax.rem(block, TILE // BLK) * BLK


def forward_kernel(slots_ref, mine_ref, q_ref, kv_hbm, out_ref, lse_ref, kv, acc, top, total, sem):
    load_by_position(slots_ref, kv_hbm, kv, sem)
    value_rows = pick(HEAD_DIM)
    for half in range(2):
        block = mine_ref[half]
        full = lax.div(block, TILE // BLK)
        top[...] = jnp.full_like(top, -1e30)
        total[...] = jnp.zeros_like(total)
        acc[...] = jnp.zeros_like(acc)

        def tile(index, masked):
            rows = pl.ds(pl.multiple_of(index * TILE, TILE), TILE)
            hide = hidden_keys(block) if masked else None
            for g in range(KV_HEADS):
                pair = kv[rows, g * PAIR : (g + 1) * PAIR]
                scores = multiply_transposed(pair, q_ref[half, g])
                if masked:
                    scores = jnp.where(hide, -1e30, scores)
                before = top[g]
                now = jnp.maximum(before, jnp.max(scores, axis=0, keepdims=True))
                weights = jnp.exp(scores - now)
                shrink = jnp.exp(before - now)
                top[g] = now
                total[g] = total[g] * shrink + jnp.sum(weights, axis=0, keepdims=True)
                turned = multiply_transposed(value_rows, pair).astype(jnp.bfloat16)
                acc[g] = acc[g] * shrink + multiply(turned, weights.astype(jnp.bfloat16))

        def step(index, _):
            tile(index, False)
            return 0

        lax.fori_loop(0, full, step, 0)
        tile(full, True)
        for g in range(KV_HEADS):
            out_ref[half, g] = acc[g] / total[g]
            lse_ref[half, g] = top[g] + jnp.log(total[g])


def backward_kernel(
    slots_ref, mine_ref, q_ref, do_ref, out_ref, lse_ref, kv_hbm, dq_ref, dkv_hbm,
    kv, grads, low, delta, acc, sem, out_sem,
):
    load_by_position(slots_ref, kv_hbm, kv, sem)
    grads[...] = jnp.zeros_like(grads)
    key_rows = pick(0)
    value_rows = pick(HEAD_DIM)
    for half in range(2):
        block = mine_ref[half]
        full = lax.div(block, TILE // BLK)
        acc[...] = jnp.zeros_like(acc)
        for g in range(KV_HEADS):
            delta[g] = jnp.sum(
                multiply_transposed(value_rows, do_ref[half, g]) * out_ref[half, g],
                axis=0,
                keepdims=True,
            )

        def tile(index, masked):
            rows = pl.ds(pl.multiple_of(index * TILE, TILE), TILE)
            hide = hidden_keys(block) if masked else None
            for g in range(KV_HEADS):
                pair = kv[rows, g * PAIR : (g + 1) * PAIR]
                scores = multiply_transposed(pair, q_ref[half, g])
                weights = jnp.exp(scores - lse_ref[half, g])
                if masked:
                    weights = jnp.where(hide, 0.0, weights)
                grad_weights = multiply_transposed(pair, do_ref[half, g])
                grad_scores = (weights * (grad_weights - delta[g])).astype(jnp.bfloat16)
                grads[rows, g * PAIR : (g + 1) * PAIR] += multiply(
                    grad_scores, q_ref[half, g]
                ) + multiply(weights.astype(jnp.bfloat16), do_ref[half, g])
                turned = multiply_transposed(key_rows, pair).astype(jnp.bfloat16)
                acc[g] += multiply(turned, grad_scores)

        def step(index, _):
            tile(index, False)
            return 0

        lax.fori_loop(0, full, step, 0)
        tile(full, True)
        dq_ref[half] = acc[...] * 0.125

    def lower(index, _):
        rows = pl.ds(pl.multiple_of(index * TILE, TILE), TILE)
        low[rows, :] = grads[rows, :].astype(jnp.bfloat16)
        return 0

    lax.fori_loop(0, low.shape[0] // TILE, lower, 0)

    def start(slot, _):
        ctx = lax.div(slot, 2)
        y, x, c = lax.div(ctx, 8), lax.rem(lax.div(ctx, 2), 4), lax.rem(ctx, 2)
        place = dkv_hbm.at[c, x * (1 - c) + y * c, y * (1 - c) + x * c]
        pltpu.make_async_copy(
            low.at[pl.ds(slots_ref[slot] * BLK, BLK)],
            place.at[pl.ds(lax.rem(slot, 2) * BLK, BLK)],
            out_sem,
        ).start()
        return 0

    lax.fori_loop(0, 64, start, 0)

    pltpu.make_async_copy(low, low, out_sem).wait()


def attend_forward(slots, mine, queries, gathered):
    smem = pl.BlockSpec(memory_space=pltpu.SMEM)
    vmem = pl.BlockSpec(memory_space=pltpu.VMEM)
    length, width = gathered.shape[0] * BLK, gathered.shape[2]
    return pl.pallas_call(
        forward_kernel,
        out_shape=(
            jax.ShapeDtypeStruct((2, KV_HEADS, HEAD_DIM, LANES), jnp.float32),
            jax.ShapeDtypeStruct((2, KV_HEADS, 1, LANES), jnp.float32),
        ),
        in_specs=[smem, smem, vmem, pl.BlockSpec(memory_space=pl.ANY)],
        out_specs=(vmem, vmem),
        scratch_shapes=[
            pltpu.VMEM((length, width), jnp.bfloat16),
            pltpu.VMEM((KV_HEADS, HEAD_DIM, LANES), jnp.float32),
            pltpu.VMEM((KV_HEADS, 1, LANES), jnp.float32),
            pltpu.VMEM((KV_HEADS, 1, LANES), jnp.float32),
            pltpu.SemaphoreType.DMA,
        ],
        compiler_params=pltpu.CompilerParams(vmem_limit_bytes=48 * 2**20),
        cost_estimate=pl.CostEstimate(
            flops=10_000_000_000, bytes_accessed=8_000_000, transcendentals=5_000_000
        ),
    )(slots, mine, queries, gathered)


def attend_backward(slots, mine, queries, grad_out, out, lse, gathered):
    smem = pl.BlockSpec(memory_space=pltpu.SMEM)
    vmem = pl.BlockSpec(memory_space=pltpu.VMEM)
    hbm = pl.BlockSpec(memory_space=pl.ANY)
    length, width = gathered.shape[0] * BLK, gathered.shape[2]
    return pl.pallas_call(
        backward_kernel,
        out_shape=(
            jax.ShapeDtypeStruct((2, KV_HEADS, HEAD_DIM, LANES), jnp.float32),
            jax.ShapeDtypeStruct((2, 4, 4, 2 * BLK, width), jnp.bfloat16),
        ),
        in_specs=[smem, smem, vmem, vmem, vmem, vmem, hbm],
        out_specs=(vmem, hbm),
        scratch_shapes=[
            pltpu.VMEM((length, width), jnp.bfloat16),
            pltpu.VMEM((length, width), jnp.float32),
            pltpu.VMEM((length, width), jnp.bfloat16),
            pltpu.VMEM((KV_HEADS, 1, LANES), jnp.float32),
            pltpu.VMEM((KV_HEADS, HEAD_DIM, LANES), jnp.float32),
            pltpu.SemaphoreType.DMA,
            pltpu.SemaphoreType.DMA,
        ],
        compiler_params=pltpu.CompilerParams(vmem_limit_bytes=48 * 2**20),
        cost_estimate=pl.CostEstimate(
            flops=20_000_000_000, bytes_accessed=12_000_000, transcendentals=5_000_000
        ),
    )(slots, mine, queries, grad_out, out, lse, gathered)


def by_group(values, before):
    parts = values.reshape(2, BLK, KV_HEADS, GROUP, HEAD_DIM).transpose(0, 2, 3, 1, 4)
    parts = parts.reshape(2, KV_HEADS, GROUP * BLK, HEAD_DIM).astype(jnp.bfloat16)
    return jnp.pad(
        parts,
        ((0, 0), (0, 0), (0, LANES - GROUP * BLK), (before, PAIR - HEAD_DIM - before)),
    )


def from_group(turned):
    parts = turned[..., : GROUP * BLK].reshape(2, KV_HEADS, HEAD_DIM, GROUP, BLK)
    return parts.transpose(0, 4, 1, 3, 2).reshape(2 * BLK, HEADS, HEAD_DIM)


MESH_IDS = pl.DeviceIdType.MESH


def remote(source, target, send_sem, recv_sem, device):
    return pltpu.make_async_remote_copy(
        src_ref=source,
        dst_ref=target,
        send_sem=send_sem,
        recv_sem=recv_sem,
        device_id=device,
        device_id_type=MESH_IDS,
    )


def greet(devices):
    barrier = pltpu.get_barrier_semaphore()
    for device in devices:
        pl.semaphore_signal(barrier, inc=1, device_id=device, device_id_type=MESH_IDS)
    pl.semaphore_wait(barrier, len(devices))


def ffn_kernel(
    h_ref, cot_columns_ref, gate_up_ref, down_ref,
    dh_ref, partial_ref, grads_ref,
    rows, cot_ref, grad, hid, dgate, dup, mine, from_sibling, kept, halves, passed, arrived,
    gather_send, gather_recv, sib_send, sib_recv, ring_send, ring_recv,
):
    x, c = lax.axis_index("x"), lax.axis_index("c")
    right, left, across = lax.rem(x + 1, 4), lax.rem(x + 3, 4), lax.rem(x + 2, 4)
    other = 1 - c
    to_right, to_left, to_sibling = {"x": right}, {"x": left}, {"c": other}
    half = BLK
    top, low = pl.ds(0, half), pl.ds(half, half)
    greet((to_right, to_left, to_sibling))

    rows[x, c] = h_ref[...]
    spot = rows.at[x, c]
    first = [
        remote(spot, spot, gather_send.at[0], gather_recv.at[0], to_right),
        remote(spot, spot, gather_send.at[1], gather_recv.at[1], to_left),
        remote(spot, spot, sib_send.at[0], sib_recv.at[0], to_sibling),
    ]
    for copy in first:
        copy.start()
    from_left, from_right, from_far = rows.at[left, c], rows.at[right, c], rows.at[across, c]
    place = lax.broadcasted_iota(jnp.int32, (2 * BLK, 2 * BLK), 0)
    across_place = lax.broadcasted_iota(jnp.int32, (2 * BLK, 2 * BLK), 1)
    identity = jnp.where(place == across_place, 1.0, 0.0).astype(jnp.bfloat16)
    for chip in range(4):
        for core in range(2):
            turned = multiply_transposed(identity, cot_columns_ref[chip, core])
            cot_ref[chip, core] = turned.astype(jnp.bfloat16)
    gate_w, up_w = gate_up_ref[0], gate_up_ref[1]
    down_w = down_ref[...]

    def work(chip, step):
        block = rows[chip].reshape(4 * BLK, D)
        gate = multiply(block, gate_w)
        up = multiply(block, up_w)
        grad_hidden = multiply_transposed(cot_ref[chip].reshape(4 * BLK, D), down_w)
        sigmoid = 1.0 / (1.0 + jnp.exp(-gate))
        silu = gate * sigmoid
        hidden = (silu * up).astype(jnp.bfloat16)
        grad_gate = (grad_hidden * up * sigmoid * (1.0 + gate * (1.0 - sigmoid))).astype(jnp.bfloat16)
        grad_up = (grad_hidden * silu).astype(jnp.bfloat16)
        hid[chip] = hidden
        dgate[chip] = grad_gate
        dup[chip] = grad_up
        grad_rows = multiply_transposed(grad_gate, gate_w) + multiply_transposed(grad_up, up_w)
        kept[step] = grad_rows.reshape(2, 2 * BLK, D)
        mine[step] = kept[step, other].astype(jnp.bfloat16)
        copy = remote(
            mine.at[step], from_sibling.at[step], sib_send.at[4 + step], sib_recv.at[4 + step], to_sibling
        )
        copy.start()
        partial_ref[chip] = multiply(hidden, down_w).astype(jnp.bfloat16).reshape(2, 2 * BLK, D)
        return copy

    first[2].wait_recv()
    backs = [work(x, 0)]
    first[0].wait_recv()
    forward_right = remote(
        from_left.at[top], from_left.at[top], gather_send.at[2], gather_recv.at[2], to_right
    )
    forward_right.start()
    sib_left = remote(from_left, from_left, sib_send.at[1], sib_recv.at[1], to_sibling)
    sib_left.start()
    first[1].wait_recv()
    forward_left = remote(
        from_right.at[low], from_right.at[low], gather_send.at[3], gather_recv.at[3], to_left
    )
    forward_left.start()
    sib_right = remote(from_right, from_right, sib_send.at[2], sib_recv.at[2], to_sibling)
    sib_right.start()
    sib_left.wait_recv()
    backs.append(work(left, 1))
    sib_right.wait_recv()
    backs.append(work(right, 2))
    forward_right.wait_recv()
    forward_left.wait_recv()
    sib_far = remote(from_far, from_far, sib_send.at[3], sib_recv.at[3], to_sibling)
    sib_far.start()
    sib_far.wait_recv()
    backs.append(work(across, 3))

    backs[3].wait_recv()
    far = kept[3, c] + from_sibling[3].astype(jnp.float32)
    halves[...] = far.astype(jnp.bfloat16)
    far_right = remote(halves.at[top], arrived.at[0, top], ring_send.at[0], ring_recv.at[0], to_right)
    far_left = remote(halves.at[low], arrived.at[0, low], ring_send.at[1], ring_recv.at[1], to_left)
    far_right.start()
    far_left.start()
    unit = FF // 32
    slabs = [(z, y) for z in range(4) for y in range(4)]

    def keep(start, down):
        for z, y in slabs:
            line, column = (z, y) if down else (y, z)
            piece = grad[
                line * unit : (line + 1) * unit, column * (D // 4) : (column + 1) * (D // 4)
            ]
            grads_ref[z, y, start : start + unit] = piece.astype(jnp.bfloat16)

    grad[...] = contract_rows(
        dgate[...].reshape(16 * BLK, FF // 8), rows[...].reshape(16 * BLK, D)
    )
    keep(0, False)
    for step in range(3):
        backs[step].wait_recv()
        kept[step, c] += from_sibling[step].astype(jnp.float32)
    far_right.wait_recv()
    passed[0, top] = (kept[2, c, top] + arrived[0, top].astype(jnp.float32)).astype(jnp.bfloat16)
    passed[0, low] = kept[2, c, low].astype(jnp.bfloat16)
    near_right = remote(passed.at[0], arrived.at[1], ring_send.at[2], ring_recv.at[2], to_right)
    near_right.start()
    far_left.wait_recv()
    passed[1, top] = kept[1, c, top].astype(jnp.bfloat16)
    passed[1, low] = (kept[1, c, low] + arrived[0, low].astype(jnp.float32)).astype(jnp.bfloat16)
    near_left = remote(passed.at[1], arrived.at[2], ring_send.at[3], ring_recv.at[3], to_left)
    near_left.start()
    grad[...] = contract_rows(
        dup[...].reshape(16 * BLK, FF // 8), rows[...].reshape(16 * BLK, D)
    )
    keep(unit, False)
    grad[...] = contract_rows(
        hid[...].reshape(16 * BLK, FF // 8), cot_ref[...].reshape(16 * BLK, D)
    )
    keep(2 * unit, True)
    near_right.wait_recv()
    near_left.wait_recv()
    dh_ref[...] = (
        kept[0, c] + arrived[1].astype(jnp.float32) + arrived[2].astype(jnp.float32)
    )
    for copy in first + [forward_right, forward_left, sib_left, sib_right, sib_far]:
        copy.wait_send()
    for copy in backs + [far_right, far_left, near_right, near_left]:
        copy.wait_send()


def feed_forward(normed, team_cotangent, gate_up, down):
    vmem = pl.BlockSpec(memory_space=pltpu.VMEM)
    width = FF // 8
    return pl.pallas_call(
        ffn_kernel,
        out_shape=(
            jax.ShapeDtypeStruct((2 * BLK, D), jnp.float32),
            jax.ShapeDtypeStruct((4, 2, 2 * BLK, D), jnp.bfloat16),
            jax.ShapeDtypeStruct((4, 4, 3 * FF // 32, D // 4), jnp.bfloat16),
        ),
        in_specs=[vmem] * 4,
        out_specs=(vmem,) * 3,
        scratch_shapes=[
            pltpu.VMEM((4, 2, 2 * BLK, D), jnp.bfloat16),
            pltpu.VMEM((4, 2, 2 * BLK, D), jnp.bfloat16),
            pltpu.VMEM((width, D), jnp.float32),
            pltpu.VMEM((4, 4 * BLK, width), jnp.bfloat16),
            pltpu.VMEM((4, 4 * BLK, width), jnp.bfloat16),
            pltpu.VMEM((4, 4 * BLK, width), jnp.bfloat16),
            pltpu.VMEM((4, 2 * BLK, D), jnp.bfloat16),
            pltpu.VMEM((4, 2 * BLK, D), jnp.bfloat16),
            pltpu.VMEM((4, 2, 2 * BLK, D), jnp.float32),
            pltpu.VMEM((2 * BLK, D), jnp.bfloat16),
            pltpu.VMEM((2, 2 * BLK, D), jnp.bfloat16),
            pltpu.VMEM((3, 2 * BLK, D), jnp.bfloat16),
            pltpu.SemaphoreType.DMA((4,)),
            pltpu.SemaphoreType.DMA((4,)),
            pltpu.SemaphoreType.DMA((8,)),
            pltpu.SemaphoreType.DMA((8,)),
            pltpu.SemaphoreType.DMA((4,)),
            pltpu.SemaphoreType.DMA((4,)),
        ],
        compiler_params=pltpu.CompilerParams(
            collective_id=1, has_side_effects=True, vmem_limit_bytes=56 * 2**20
        ),
        cost_estimate=pl.CostEstimate(
            flops=6_000_000_000, bytes_accessed=12_000_000, transcendentals=400_000
        ),
    )(normed, team_cotangent, gate_up, down)


def ring_of(axis):
    place = lax.axis_index(axis)
    return place, {axis: lax.rem(place + 1, 4)}, {axis: lax.rem(place + 3, 4)}


def plane_rings():
    x, y, c = lax.axis_index("x"), lax.axis_index("y"), lax.axis_index("c")

    def along(step_x, step_y):
        return {"y": lax.rem(y + step_y, 4), "x": lax.rem(x + step_x, 4)}

    first = (x * (1 - c) + y * c, along(1 - c, c), along(3 * (1 - c), 3 * c))
    second = (y * (1 - c) + x * c, along(c, 1 - c), along(3 * c, 3 * (1 - c)))
    return first, second


def cut(rows):
    top = (rows // 2 + 15) // 16 * 16
    return pl.ds(0, top), pl.ds(top, rows - top)


class RingGather:
    def __init__(self, ring, own, spot, parts, send, recv):
        self.place, self.right, self.left = ring
        self.own, self.spot, self.parts, self.send, self.recv = own, spot, parts, send, recv
        self.begun = []

    def _go(self, source, target, index, device):
        copy = remote(source, target, self.send.at[index], self.recv.at[index], device)
        copy.start()
        self.begun.append(copy)
        return copy

    def near(self):
        target = self.spot(self.place)
        self.to_right = self._go(self.own, target, 0, self.right)
        self.to_left = self._go(self.own, target, 1, self.left)

    def from_left(self):
        self.to_right.wait_recv()
        block = self.spot(lax.rem(self.place + 3, 4))
        piece = block.at[self.parts[0]]
        self.on_right = self._go(piece, piece, 2, self.right)
        return block

    def from_right(self):
        self.to_left.wait_recv()
        block = self.spot(lax.rem(self.place + 1, 4))
        piece = block.at[self.parts[1]]
        self.on_left = self._go(piece, piece, 3, self.left)
        return block

    def from_far(self):
        self.on_right.wait_recv()
        self.on_left.wait_recv()
        return self.spot(lax.rem(self.place + 2, 4))

    def drain(self):
        for copy in self.begun:
            copy.wait_send()


class Passing:
    def __init__(self, send, recv):
        self.send, self.recv, self.copies = send, recv, []
        self.device = {"c": 1 - lax.axis_index("c")}

    def go(self, source, target):
        k = len(self.copies)
        copy = remote(source, target, self.send.at[k], self.recv.at[k], self.device)
        copy.start()
        self.copies.append(copy)

    def wait(self):
        for copy in self.copies:
            copy.wait_recv()

    def drain(self):
        for copy in self.copies:
            copy.wait_send()


def first_gather_kernel(
    w_ref, gain_ref, w_out, gain_out,
    w_send, w_recv, gain_send, gain_recv, sib_send, sib_recv, local,
):
    c = lax.axis_index("c")
    z_ring = ring_of("z")
    greet((z_ring[1], z_ring[2], {"c": 1 - c}))
    passing = Passing(sib_send, sib_recv)
    weights = RingGather(
        z_ring, w_ref.at[c], lambda i: w_out.at[c, i], cut(w_ref.shape[1]), w_send, w_recv
    )
    gains = RingGather(
        z_ring, gain_ref, lambda i: gain_out.at[i], cut(gain_ref.shape[0]), gain_send, gain_recv
    )
    weights.near()
    gains.near()
    z = z_ring[0]
    own = [
        pltpu.make_async_copy(w_ref, w_out.at[:, z], local.at[0]),
        pltpu.make_async_copy(gain_ref, gain_out.at[z], local.at[1]),
    ]
    for copy in own:
        copy.start()
    for turn in ("from_left", "from_right", "from_far"):
        block = getattr(weights, turn)()
        passing.go(block, block)
        getattr(gains, turn)()
    passing.wait()
    for copy in own:
        copy.wait()
    weights.drain()
    gains.drain()
    passing.drain()


def second_gather_kernel(
    kv_ref, o_ref, down_ref, kv_out, o_out, down_out,
    kv_send, kv_recv, o_send, o_recv, down_send, down_recv, sib_send, sib_recv, o_sib_send, o_sib_recv, local,
):
    x, y, c = lax.axis_index("x"), lax.axis_index("y"), lax.axis_index("c")
    z_ring = ring_of("z")
    first, second = plane_rings()
    greet((first[1], first[2], second[1], second[2], z_ring[1], z_ring[2], {"c": 1 - c}))
    a0 = first[0]

    def spot(a, b):
        return kv_out.at[b * (1 - c) + a * c, a * (1 - c) + b * c, c]

    rows = cut(kv_ref.shape[0])
    passing = Passing(sib_send, sib_recv)
    o_passing = Passing(o_sib_send, o_sib_recv)

    def hand(block):
        passing.go(block, block)

    stage = RingGather(
        first, kv_ref, lambda a: spot(a, second[0]), rows, kv_send.at[0], kv_recv.at[0]
    )

    def spread_ring(k, shift, own):
        a = lax.rem(a0 + shift, 4)
        ring = RingGather(
            second, own, lambda b: spot(a, b), rows, kv_send.at[1 + k], kv_recv.at[1 + k]
        )
        ring.near()
        return ring

    stage.near()
    ring_own = spread_ring(0, 0, kv_ref)
    passing.go(kv_ref, spot(a0, second[0]))
    z_rings = (
        RingGather(z_ring, o_ref.at[c], lambda i: o_out.at[c, i], cut(o_ref.shape[1]), o_send, o_recv),
        RingGather(z_ring, down_ref, lambda i: down_out.at[i], cut(down_ref.shape[0]), down_send, down_recv),
    )
    for ring in z_rings:
        ring.near()
    z = z_ring[0]
    own = [
        pltpu.make_async_copy(kv_ref, kv_out.at[y, x, c], local.at[0]),
        pltpu.make_async_copy(o_ref, o_out.at[:, z], local.at[1]),
        pltpu.make_async_copy(down_ref, down_out.at[z], local.at[2]),
    ]
    for copy in own:
        copy.start()
    block = stage.from_left()
    ring_left = spread_ring(1, 3, block)
    hand(block)
    block = stage.from_right()
    ring_right = spread_ring(2, 1, block)
    hand(block)
    block = stage.from_far()
    ring_far = spread_ring(3, 2, block)
    hand(block)
    plane = (ring_own, ring_left, ring_right, ring_far)
    for turn in ("from_left", "from_right"):
        for ring in plane:
            hand(getattr(ring, turn)())
        block = getattr(z_rings[0], turn)()
        o_passing.go(block, block)
        getattr(z_rings[1], turn)()
    for ring in plane:
        hand(ring.from_far())
    block = z_rings[0].from_far()
    o_passing.go(block, block)
    z_rings[1].from_far()
    passing.wait()
    o_passing.wait()
    for copy in own:
        copy.wait()
    for ring in (stage,) + plane + z_rings:
        ring.drain()
    passing.drain()
    o_passing.drain()


def dma(*counts):
    return [pltpu.SemaphoreType.DMA(n if isinstance(n, tuple) else (n,)) for n in counts]


def first_gather(weights, gains):
    hbm = pl.BlockSpec(memory_space=pl.ANY)
    return pl.pallas_call(
        first_gather_kernel,
        out_shape=(
            jax.ShapeDtypeStruct((2, 4) + weights.shape[1:], weights.dtype),
            jax.ShapeDtypeStruct((4,) + gains.shape, gains.dtype),
        ),
        in_specs=[hbm] * 2,
        out_specs=(hbm,) * 2,
        scratch_shapes=dma(4, 4, 4, 4, 3, 3, 2),
        compiler_params=pltpu.CompilerParams(collective_id=2, has_side_effects=True),
        cost_estimate=pl.CostEstimate(flops=0, bytes_accessed=60_000_000, transcendentals=0),
    )(weights, gains)


def second_gather(kv, weight, down):
    hbm = pl.BlockSpec(memory_space=pl.ANY)
    return pl.pallas_call(
        second_gather_kernel,
        out_shape=(
            jax.ShapeDtypeStruct((4, 4, 2) + kv.shape, kv.dtype),
            jax.ShapeDtypeStruct((2, 4) + weight.shape[1:], weight.dtype),
            jax.ShapeDtypeStruct((4,) + down.shape, down.dtype),
        ),
        in_specs=[hbm] * 3,
        out_specs=(hbm,) * 3,
        scratch_shapes=dma((5, 4), (5, 4), 4, 4, 4, 4, 16, 16, 3, 3, 3),
        compiler_params=pltpu.CompilerParams(collective_id=3, has_side_effects=True),
        cost_estimate=pl.CostEstimate(flops=0, bytes_accessed=100_000_000, transcendentals=0),
    )(kv, weight, down)


class RingSum:
    def __init__(self, ring, value, parts, far, passed, far_in, near_in, send, recv):
        self.place, self.right, self.left = ring
        self.value, self.parts = value, parts
        self.far, self.passed, self.far_in, self.near_in = far, passed, far_in, near_in
        self.send, self.recv = send, recv
        self.begun = []

    def _go(self, source, target, index, device):
        copy = remote(source, target, self.send.at[index], self.recv.at[index], device)
        copy.start()
        self.begun.append(copy)
        return copy

    def send_far(self):
        top, low = self.parts
        other = lax.rem(self.place + 2, 4)
        for part in self.parts:
            self.far[part] = self.value(other, part).astype(jnp.bfloat16)
        self.far_right = self._go(self.far.at[top], self.far_in.at[top], 0, self.right)
        self.far_left = self._go(self.far.at[low], self.far_in.at[low], 1, self.left)

    def send_right(self):
        top, low = self.parts
        other = lax.rem(self.place + 1, 4)
        self.passed[0, low] = self.value(other, low).astype(jnp.bfloat16)
        self.far_right.wait_recv()
        total = self.value(other, top) + self.far_in[top].astype(jnp.float32)
        self.passed[0, top] = total.astype(jnp.bfloat16)
        self.near_right = self._go(self.passed.at[0], self.near_in.at[0], 2, self.right)

    def send_left(self):
        top, low = self.parts
        other = lax.rem(self.place + 3, 4)
        self.passed[1, top] = self.value(other, top).astype(jnp.bfloat16)
        self.far_left.wait_recv()
        total = self.value(other, low) + self.far_in[low].astype(jnp.float32)
        self.passed[1, low] = total.astype(jnp.bfloat16)
        self.near_left = self._go(self.passed.at[1], self.near_in.at[1], 3, self.left)

    def arrive(self):
        self.near_right.wait_recv()
        self.near_left.wait_recv()

    def total(self, part):
        return (
            self.value(self.place, part)
            + self.near_in[0, part].astype(jnp.float32)
            + self.near_in[1, part].astype(jnp.float32)
        )

    def drain(self):
        for copy in self.begun:
            copy.wait_send()


def ring_scratch(shape):
    return [
        pltpu.VMEM(shape, jnp.bfloat16),
        pltpu.VMEM((2,) + shape, jnp.bfloat16),
        pltpu.VMEM(shape, jnp.bfloat16),
        pltpu.VMEM((2,) + shape, jnp.bfloat16),
        pltpu.SemaphoreType.DMA((4,)),
        pltpu.SemaphoreType.DMA((4,)),
    ]


HALVES = (pl.ds(0, 2), pl.ds(2, 2))


class PlaneSum:
    def __init__(self, rings, parts, theirs, one, two, sib_send, sib_recv):
        self.first, self.second = rings
        self.parts, self.theirs = parts, theirs
        self.c = lax.axis_index("c")
        self.sib_send, self.sib_recv = sib_send, sib_recv
        middle, one, two = one[0], one[1:], two
        self.middle = middle
        shape = middle.shape[1:]
        self.rows = (pl.ds(0, shape[0] // 2), pl.ds(shape[0] // 2, shape[0] // 2))
        self.ring_one = RingSum(self.first, self._both, HALVES, *one)
        self.ring_two = RingSum(self.second, self._middle, self.rows, *two)

    def _both(self, a, part):
        mine = self.parts[self.c, a, part].astype(jnp.float32)
        return mine + self.theirs[a, part].astype(jnp.float32)

    def _middle(self, b, part):
        return self.middle[b, part].astype(jnp.float32)

    def hand(self, k):
        a = lax.rem(self.second[0] + (2, 1, 3, 0)[k], 4)
        copy = remote(
            self.parts.at[1 - self.c, a],
            self.theirs.at[a],
            self.sib_send.at[k],
            self.sib_recv.at[k],
            {"c": 1 - self.c},
        )
        copy.start()
        return copy

    def along_first(self, handed):
        one = self.ring_one
        handed[0].wait_recv()
        one.send_far()
        handed[1].wait_recv()
        one.send_right()
        handed[2].wait_recv()
        one.send_left()
        handed[3].wait_recv()

    def along_second(self):
        one, two = self.ring_one, self.ring_two
        one.arrive()
        for part in HALVES:
            self.middle[part] = one.total(part).astype(jnp.bfloat16)
        two.send_far()
        two.send_right()
        two.send_left()

    def drain(self, handed):
        for copy in handed:
            copy.wait_send()
        self.ring_one.drain()
        self.ring_two.drain()


ORDER = (2, 1, 3, 0)


def fill(plane, left_ref, right_ref):
    c = lax.axis_index("c")
    wide = left_ref.shape[3]

    rows = plane.parts.shape[-1]

    def product(core, a):
        lhs = left_ref[core, a].reshape(4 * wide, left_ref.shape[4])
        block = multiply(lhs, right_ref[...]).astype(jnp.bfloat16)
        for z in range(4):
            piece = block[:, z * LANES : z * LANES + rows]
            plane.parts[core, a, :, z] = piece.reshape(4, wide, rows)

    handed = []
    for k in range(4):
        product(1 - c, lax.rem(plane.second[0] + ORDER[k], 4))
        handed.append(plane.hand(k))
    for k in range(4):
        product(c, lax.rem(plane.first[0] + ORDER[k], 4))
    return handed


def pairs_sum_kernel(
    parts, ffn, left_ref, right_ref, kv_out, ffn_out, out_ref,
    theirs, middle, products, their_products, products_middle, last, *scratch,
):
    sems, rest = scratch[:4], scratch[4:]
    one, two, three, four, five, six = (rest[6 * k : 6 * k + 6] for k in range(6))
    first, second = plane_rings()
    z_ring = ring_of("z")
    greet((first[1], first[2], second[1], second[2], z_ring[1], z_ring[2], {"c": 1 - lax.axis_index("c")}))
    pairs = PlaneSum((first, second), parts, theirs, (middle,) + one, two, *sems[:2])
    weights = PlaneSum(
        (first, second), products, their_products, (products_middle,) + four, five, *sems[2:]
    )
    handed = [pairs.hand(k) for k in range(4)]
    along_z = RingSum(
        z_ring, lambda i, part: ffn[i, part].astype(jnp.float32), HALVES, *three
    )
    along_z.send_far()
    handed_weights = fill(weights, left_ref, right_ref)
    pairs.along_first(handed)
    weights.along_first(handed_weights)
    along_z.send_right()
    along_z.send_left()
    pairs.along_second()
    weights.along_second()
    pairs.ring_two.arrive()
    for part in pairs.rows:
        kv_out[part] = pairs.ring_two.total(part)
    weights.ring_two.arrive()
    for part in weights.rows:
        last[part] = weights.ring_two.total(part)
    weights_z = RingSum(z_ring, lambda i, part: last[i, part], cut(left_ref.shape[3]), *six)
    weights_z.send_far()
    along_z.arrive()
    for part in HALVES:
        ffn_out[part] = along_z.total(part).astype(jnp.bfloat16)
    weights_z.send_right()
    weights_z.send_left()
    weights_z.arrive()
    for part in weights_z.parts:
        out_ref[part] = weights_z.total(part)
    pairs.drain(handed)
    weights.drain(handed_weights)
    along_z.drain()
    weights_z.drain()


def pairs_sum(parts, ffn, left, right):
    vmem = pl.BlockSpec(memory_space=pltpu.VMEM)
    block, share = parts.shape[3:], ffn.shape[2:]
    weight = (left.shape[3], D // 4)
    return pl.pallas_call(
        pairs_sum_kernel,
        out_shape=(
            jax.ShapeDtypeStruct(block, jnp.float32),
            jax.ShapeDtypeStruct((4,) + share, jnp.bfloat16),
            jax.ShapeDtypeStruct(weight, jnp.float32),
        ),
        in_specs=[vmem] * 4,
        out_specs=(vmem,) * 3,
        scratch_shapes=[
            pltpu.VMEM((4, 4) + block, jnp.bfloat16),
            pltpu.VMEM((4,) + block, jnp.bfloat16),
            pltpu.VMEM((2, 4, 4, 4) + weight, jnp.bfloat16),
            pltpu.VMEM((4, 4, 4) + weight, jnp.bfloat16),
            pltpu.VMEM((4, 4) + weight, jnp.bfloat16),
            pltpu.VMEM((4,) + weight, jnp.float32),
        ]
        + dma(4, 4, 4, 4)
        + ring_scratch((4,) + block)
        + ring_scratch(block)
        + ring_scratch((4,) + share)
        + ring_scratch((4, 4) + weight)
        + ring_scratch((4,) + weight)
        + ring_scratch(weight),
        compiler_params=pltpu.CompilerParams(
            collective_id=4, has_side_effects=True, vmem_limit_bytes=60 * 2**20
        ),
    )(parts, ffn, left, right)


def weights_sum_kernel(
    left_ref, right_ref, ffn_ref, out_ref, ffn_out, down_out,
    parts, theirs, middle, last, down_own, *scratch,
):
    sems, rest = scratch[:2], scratch[2:]
    one, two, three, four = (rest[6 * k : 6 * k + 6] for k in range(4))
    down_send, down_recv, local = rest[24:]
    x, c = lax.axis_index("x"), lax.axis_index("c")
    first, second = plane_rings()
    z_ring, y_ring = ring_of("z"), ring_of("y")
    team = [
        {"x": lax.rem(x + step, 4), "c": (1 - c) if swap else c}
        for swap in (0, 1)
        for step in range(4)
        if step + swap > 0
    ]
    greet([y_ring[1], y_ring[2], z_ring[1], z_ring[2]] + team)
    along_y = RingSum(
        y_ring,
        lambda i, part: ffn_ref[i, part].astype(jnp.float32),
        cut(ffn_ref.shape[1]),
        *four,
    )
    along_y.send_far()
    plane = PlaneSum((first, second), parts, theirs, (middle,) + one, two, *sems)
    handed = fill(plane, left_ref, right_ref)
    along_y.send_right()
    along_y.send_left()
    plane.along_first(handed)
    along_y.arrive()
    for part in along_y.parts:
        ffn_out[part] = along_y.total(part).astype(jnp.bfloat16)
    third = down_own.shape[0]
    down_own[...] = ffn_out[2 * third : 3 * third]
    own = pltpu.make_async_copy(down_own, down_out.at[x, c], local)
    own.start()
    downs = [
        remote(down_own, down_out.at[x, c], down_send.at[k], down_recv.at[k], device)
        for k, device in enumerate(team)
    ]
    for copy in downs:
        copy.start()
    plane.along_second()
    plane.ring_two.arrive()
    for part in plane.rows:
        last[part] = plane.ring_two.total(part)
    along_z = RingSum(z_ring, lambda i, part: last[i, part], cut(left_ref.shape[3]), *three)
    along_z.send_far()
    along_z.send_right()
    along_z.send_left()
    along_z.arrive()
    for part in along_z.parts:
        out_ref[part] = along_z.total(part)
    own.wait()
    for copy in downs:
        copy.wait_recv()
    plane.drain(handed)
    along_z.drain()
    along_y.drain()
    for copy in downs:
        copy.wait_send()


def weights_sum(left, right, ffn):
    vmem = pl.BlockSpec(memory_space=pltpu.VMEM)
    hbm = pl.BlockSpec(memory_space=pl.ANY)
    block = (left.shape[3], D // 4)
    share = ffn.shape[1:]
    down = (share[0] // 3, share[1])
    return pl.pallas_call(
        weights_sum_kernel,
        out_shape=(
            jax.ShapeDtypeStruct(block, jnp.float32),
            jax.ShapeDtypeStruct(share, jnp.bfloat16),
            jax.ShapeDtypeStruct((4, 2) + down, jnp.bfloat16),
        ),
        in_specs=[vmem] * 3,
        out_specs=(vmem, vmem, hbm),
        scratch_shapes=[
            pltpu.VMEM((2, 4, 4, 4) + block, jnp.bfloat16),
            pltpu.VMEM((4, 4, 4) + block, jnp.bfloat16),
            pltpu.VMEM((4, 4) + block, jnp.bfloat16),
            pltpu.VMEM((4,) + block, jnp.float32),
            pltpu.VMEM(down, jnp.bfloat16),
        ]
        + dma(4, 4)
        + ring_scratch((4, 4) + block)
        + ring_scratch((4,) + block)
        + ring_scratch(block)
        + ring_scratch(share)
        + dma(7, 7)
        + [pltpu.SemaphoreType.DMA],
        compiler_params=pltpu.CompilerParams(
            collective_id=5, has_side_effects=True, vmem_limit_bytes=60 * 2**20
        ),
    )(left, right, ffn)


def shards(
    tokens, cotangent, slot_blocks, norm_gains,
    w_query, w_key, w_value, w_output, w_gate, w_up, w_down,
):
    inputs = tokens[0].astype(jnp.float32)
    row_count = inputs.shape[0]
    ctx_index = lax.axis_index(CTX)
    member = lax.axis_index(TEAM)
    mine = lax.dynamic_slice_in_dim(slot_blocks, 2 * ctx_index, 2)
    offsets = jnp.arange(BLK, dtype=jnp.int32)
    local_pos = (mine[:, None] * BLK + offsets[None, :]).reshape(row_count)
    cosine, sine = rope_tables(local_pos)

    kv_parts = [
        w[:, h * HEAD_DIM : (h + 1) * HEAD_DIM] for h in range(KV_HEADS) for w in (w_key, w_value)
    ]
    w_kv = jnp.concatenate(kv_parts, axis=1)
    wide = w_kv.shape[1] // 2
    gain_rows = jnp.pad(norm_gains, (0, 32 * 128 - norm_gains.shape[0])).reshape(32, 128)
    full_kv, gains = first_gather(jnp.stack([w_kv[:, :wide], w_kv[:, wide:]]), gain_rows)
    full_kv = full_kv.reshape(2, D, wide)
    gains = gains.reshape(4, -1)[:, : D // 2].reshape(2 * D).astype(jnp.float32)

    source = jnp.arange(FF // 8, dtype=jnp.int32)
    source = source // (FF // 32) * (FF // 4) + member * (FF // 32) + source % (FF // 32)
    picked = (jnp.arange(FF, dtype=jnp.int32)[:, None] == source[None, :]).astype(jnp.bfloat16)
    my_gate_up = jnp.stack(
        [multiply(w_gate, picked).astype(jnp.bfloat16), multiply(w_up, picked).astype(jnp.bfloat16)]
    )
    my_down = lax.dynamic_slice_in_dim(w_down, member * (FF // 32), FF // 32)
    upstream_low = cotangent[0]
    gate_up = lax.all_gather(my_gate_up, "z", axis=1, tiled=True)
    full_output = lax.all_gather(w_output, "z", axis=0, tiled=True)
    team_upstream = lax.all_gather(cotangent, TEAM, axis=0, tiled=True)
    my_query = jnp.stack([w_query[:, : D // 2], w_query[:, D // 2 :]])
    gain_first, gain_second = gains[:D], gains[D:]

    root_first = lax.rsqrt(jnp.mean(inputs * inputs, axis=-1, keepdims=True) + epsilon)
    normed_first = (inputs * root_first * gain_first).astype(jnp.bfloat16)
    raw_kv = jnp.concatenate(
        [multiply(normed_first, full_kv[0]), multiply(normed_first, full_kv[1])], axis=1
    )
    pairs = raw_kv.reshape(row_count, KV_HEADS, 2, HEAD_DIM)
    keys = rotate(pairs[:, :, 0], cosine, sine)
    packed = jnp.stack([keys, pairs[:, :, 1]], axis=2).astype(jnp.bfloat16)
    packed = packed.reshape(row_count, KV_HEADS * PAIR)
    gathered, full_query, down = second_gather(packed, my_query, my_down)
    down = down.reshape(FF // 8, D)
    gathered = gathered.reshape(64, BLK, KV_HEADS * PAIR)
    full_query = full_query.reshape(2, D, D // 2)
    raw = jnp.concatenate(
        [multiply(normed_first, full_query[0]), multiply(normed_first, full_query[1])], axis=1
    )
    queries = rotate(raw.reshape(row_count, HEADS, HEAD_DIM), cosine, sine)
    query_rows = by_group(queries.astype(jnp.bfloat16) * jnp.bfloat16(0.125), 0)
    out_turned, lse = attend_forward(slot_blocks, mine, query_rows, gathered)
    attended = from_group(out_turned).reshape(row_count, D).astype(jnp.bfloat16)
    middle = inputs + multiply(attended, full_output)

    root_second = lax.rsqrt(jnp.mean(middle * middle, axis=-1, keepdims=True) + epsilon)
    normed_second = (middle * root_second * gain_second).astype(jnp.bfloat16)
    grad_normed_second, partial, grad_ffn = feed_forward(
        normed_second,
        team_upstream.swapaxes(1, 2).reshape(4, 2, D, row_count),
        gate_up,
        down,
    )
    down_sum = lax.psum_scatter(
        partial.reshape(8, row_count, D), TEAM, scatter_dimension=0, tiled=True
    )

    norm_part, gain_grad_second = norm_backward(
        grad_normed_second, middle, root_second, gain_second
    )
    grad_middle = upstream_low.astype(jnp.float32) + norm_part
    middle_low = grad_middle.astype(jnp.bfloat16)

    grad_attended = multiply_transposed(middle_low, full_output).astype(jnp.bfloat16)

    grad_rows = by_group(grad_attended.reshape(row_count, HEADS, HEAD_DIM), HEAD_DIM)
    query_turned, grad_pairs = attend_backward(
        slot_blocks, mine, query_rows, grad_rows, out_turned, lse, gathered
    )
    grad_query_raw = rotate(from_group(query_turned), cosine, -sine)
    grad_query_raw = grad_query_raw.reshape(row_count, D).astype(jnp.bfloat16)

    def by_owner(columns):
        columns = columns.reshape((4, 4, 2) + columns.shape[1:])
        return jnp.stack([columns[:, :, 0].swapaxes(0, 1), columns[:, :, 1]])

    above = jnp.pad(grad_query_raw.reshape(row_count, 32, 30), ((0, 0), (0, 0), (0, 34)))
    below = jnp.pad(middle_low.reshape(row_count, 32, 30), ((0, 0), (0, 0), (30, 4)))
    columns = by_owner(jnp.concatenate([above, below], axis=0).transpose(1, 2, 0))

    def by_rows(values):
        parts = values.reshape(-1, 4, D // 4)
        return jnp.pad(parts, ((0, 0), (0, 0), (0, LANES - D // 4))).reshape(-1, 4 * LANES)

    normed_rows = by_rows(normed_first)
    rows = jnp.concatenate([normed_rows, by_rows(attended)], axis=0)
    own_pairs, part_ffn, sum_query_output = pairs_sum(grad_pairs, grad_ffn, columns, rows)
    own_pairs = own_pairs.reshape(row_count, KV_HEADS, 2, HEAD_DIM)
    grad_key_raw = rotate(own_pairs[:, :, 0], cosine, -sine)
    grad_kv = jnp.stack([grad_key_raw, own_pairs[:, :, 1]], axis=2)
    grad_kv = grad_kv.reshape(row_count, -1).astype(jnp.bfloat16)
    grad_normed_first = multiply_transposed(grad_query_raw[:, : D // 2], full_query[0])
    grad_normed_first += multiply_transposed(grad_query_raw[:, D // 2 :], full_query[1])
    grad_normed_first += multiply_transposed(grad_kv[:, :wide], full_kv[0])
    grad_normed_first += multiply_transposed(grad_kv[:, wide:], full_kv[1])
    norm_first_part, gain_grad_first = norm_backward(
        grad_normed_first, inputs, root_first, gain_first
    )
    input_grad = grad_middle + norm_first_part

    kv_columns = grad_kv.reshape(row_count, KV_HEADS, 2, HEAD_DIM)
    k_columns = kv_columns[:, :, 0].reshape(row_count, 32, 10)
    v_columns = kv_columns[:, :, 1].reshape(row_count, 32, 10)
    columns = jnp.concatenate([k_columns, v_columns], axis=2)
    columns = jnp.pad(columns, ((0, 0), (0, 0), (0, 12))).transpose(1, 2, 0)
    owners = jnp.arange(32, dtype=jnp.int32)
    mark = (owners[:, None, None] == owners[None, None, :]) & (owners[None, :, None] == 20)
    columns = jnp.concatenate([columns, mark.astype(jnp.bfloat16)], axis=2)
    gain_rows = jnp.concatenate([gain_grad_first, gain_grad_second]).astype(jnp.bfloat16)
    gain_rows = jnp.pad(gain_rows.reshape(32, 4, 15), ((0, 0), (0, 0), (0, LANES - 15)))
    sum_pair, sum_ffn, team_down = weights_sum(
        by_owner(columns),
        jnp.concatenate([normed_rows, gain_rows.reshape(32, 4 * LANES)], axis=0),
        part_ffn,
    )
    down_sum, sum_pair = lax.optimization_barrier((down_sum, sum_pair))
    layer_out = (middle + down_sum[0].astype(jnp.float32)).astype(jnp.bfloat16)[None]
    sum_query_output, sum_pair = sum_query_output.T, sum_pair.T
    ffn_columns = sum_ffn[:160].T.astype(jnp.float32)
    sum_down = lax.dynamic_slice_in_dim(
        team_down.reshape(FF // 4, D // 4), member * 30, 30, axis=1
    ).astype(jnp.float32)
    return (
        layer_out,
        input_grad[None],
        sum_pair[:15, 20],
        sum_query_output[:, :30],
        sum_pair[:, :10],
        sum_pair[:, 10:20],
        sum_query_output[:, 30:60],
        ffn_columns[:, :80],
        ffn_columns[:, 80:],
        sum_down,
    )


def solution(mesh):
    fine = Mesh(mesh.devices.reshape(4, 4, 2, 4), ALL)
    weight = P("z", None)
    return jax.shard_map(
        shards,
        mesh=fine,
        in_specs=(
            P("z", CTX, None),
            P("z", CTX, None),
            P(),
            P("z"),
        )
        + (weight,) * 7,
        out_specs=(
            P("z", CTX, None),
            P("z", CTX, None),
            P(ALL),
        )
        + (P("z", CTX),) * 7,
        check_vma=False,
    )
```

```python
import math

import jax
import jax.numpy as jnp
from jax import lax
from jax.experimental import pallas as pl
from jax.experimental.pallas import tpu as pltpu
from jax.sharding import Mesh
from jax.sharding import PartitionSpec as P

HEADS = 15
KV_HEADS = 5
HEAD_DIM = 64
GROUP = HEADS // KV_HEADS
BLK = 64
TILE = 512
PAIR = 2 * HEAD_DIM
LANES = 256
D = 960
FF = 2560
CTX = ("y", "x", "c")
ALL = ("y", "x", "c", "z")
TEAM = ("x", "c")

epsilon = 1e-05
NT = (((1,), (1,)), ((), ()))


def multiply(left, right):
    return jnp.dot(left, right, preferred_element_type=jnp.float32)


def multiply_transposed(left, right):
    return lax.dot_general(left, right, NT, preferred_element_type=jnp.float32)


def contract_rows(left, right):
    return lax.dot_general(
        left, right, (((0,), (0,)), ((), ())), preferred_element_type=jnp.float32
    )


def rope_tables(positions):
    counter = jnp.arange(HEAD_DIM // 2, dtype=jnp.float32)
    frequency = jnp.exp(counter * (-2.0 * math.log(10000.0) / HEAD_DIM))
    angles = positions.astype(jnp.float32)[:, None] * frequency[None, :]
    return (jnp.cos(angles), jnp.sin(angles))


def rotate(values, cosine, sine):
    half = HEAD_DIM // 2
    first, second = values[..., :half], values[..., half:]
    cos_rows, sin_rows = cosine[:, None, :], sine[:, None, :]
    return jnp.concatenate(
        [first * cos_rows - second * sin_rows, second * cos_rows + first * sin_rows], axis=-1
    )


def norm_backward(grad_normed, values, inverse_root, gain):
    gain_grad = jnp.sum(grad_normed * values * inverse_root, axis=0)
    scaled = grad_normed * gain
    value_grad = inverse_root * scaled - values * inverse_root**3 * jnp.mean(
        scaled * values, axis=-1, keepdims=True
    )
    return (value_grad, gain_grad)


def load_by_position(slots_ref, kv_hbm, kv, sem):
    def start(slot, _):
        pltpu.make_async_copy(
            kv_hbm.at[slot], kv.at[pl.ds(slots_ref[slot] * BLK, BLK)], sem
        ).start()
        return 0

    lax.fori_loop(0, 64, start, 0)

    pltpu.make_async_copy(kv, kv, sem).wait()


def pick(offset):
    row = lax.broadcasted_iota(jnp.int32, (HEAD_DIM, PAIR), 0)
    lane = lax.broadcasted_iota(jnp.int32, (HEAD_DIM, PAIR), 1)
    return jnp.where(lane == row + offset, 1.0, 0.0).astype(jnp.bfloat16)


def hidden_keys(block):
    key = lax.broadcasted_iota(jnp.int32, (TILE, LANES), 0)
    lane = lax.broadcasted_iota(jnp.int32, (TILE, LANES), 1)
    return key > lax.rem(lane, BLK) + lax.rem(block, TILE // BLK) * BLK


def forward_kernel(slots_ref, mine_ref, q_ref, kv_hbm, out_ref, lse_ref, kv, acc, top, total, sem):
    load_by_position(slots_ref, kv_hbm, kv, sem)
    value_rows = pick(HEAD_DIM)
    for half in range(2):
        block = mine_ref[half]
        full = lax.div(block, TILE // BLK)
        top[...] = jnp.full_like(top, -1e30)
        total[...] = jnp.zeros_like(total)
        acc[...] = jnp.zeros_like(acc)

        def tile(index, masked):
            rows = pl.ds(pl.multiple_of(index * TILE, TILE), TILE)
            hide = hidden_keys(block) if masked else None
            for g in range(KV_HEADS):
                pair = kv[rows, g * PAIR : (g + 1) * PAIR]
                scores = multiply_transposed(pair, q_ref[half, g])
                if masked:
                    scores = jnp.where(hide, -1e30, scores)
                before = top[g]
                now = jnp.maximum(before, jnp.max(scores, axis=0, keepdims=True))
                weights = jnp.exp(scores - now)
                shrink = jnp.exp(before - now)
                top[g] = now
                total[g] = total[g] * shrink + jnp.sum(weights, axis=0, keepdims=True)
                turned = multiply_transposed(value_rows, pair).astype(jnp.bfloat16)
                acc[g] = acc[g] * shrink + multiply(turned, weights.astype(jnp.bfloat16))

        def step(index, _):
            tile(index, False)
            return 0

        lax.fori_loop(0, full, step, 0)
        tile(full, True)
        for g in range(KV_HEADS):
            out_ref[half, g] = acc[g] / total[g]
            lse_ref[half, g] = top[g] + jnp.log(total[g])


def backward_kernel(
    slots_ref, mine_ref, q_ref, do_ref, out_ref, lse_ref, kv_hbm, dq_ref, dkv_hbm,
    kv, grads, low, delta, acc, sem, out_sem,
):
    load_by_position(slots_ref, kv_hbm, kv, sem)
    grads[...] = jnp.zeros_like(grads)
    key_rows = pick(0)
    value_rows = pick(HEAD_DIM)
    for half in range(2):
        block = mine_ref[half]
        full = lax.div(block, TILE // BLK)
        acc[...] = jnp.zeros_like(acc)
        for g in range(KV_HEADS):
            delta[g] = jnp.sum(
                multiply_transposed(value_rows, do_ref[half, g]) * out_ref[half, g],
                axis=0,
                keepdims=True,
            )

        def tile(index, masked):
            rows = pl.ds(pl.multiple_of(index * TILE, TILE), TILE)
            hide = hidden_keys(block) if masked else None
            for g in range(KV_HEADS):
                pair = kv[rows, g * PAIR : (g + 1) * PAIR]
                scores = multiply_transposed(pair, q_ref[half, g])
                weights = jnp.exp(scores - lse_ref[half, g])
                if masked:
                    weights = jnp.where(hide, 0.0, weights)
                grad_weights = multiply_transposed(pair, do_ref[half, g])
                grad_scores = (weights * (grad_weights - delta[g])).astype(jnp.bfloat16)
                grads[rows, g * PAIR : (g + 1) * PAIR] += multiply(
                    grad_scores, q_ref[half, g]
                ) + multiply(weights.astype(jnp.bfloat16), do_ref[half, g])
                turned = multiply_transposed(key_rows, pair).astype(jnp.bfloat16)
                acc[g] += multiply(turned, grad_scores)

        def step(index, _):
            tile(index, False)
            return 0

        lax.fori_loop(0, full, step, 0)
        tile(full, True)
        dq_ref[half] = acc[...] * 0.125

    def lower(index, _):
        rows = pl.ds(pl.multiple_of(index * TILE, TILE), TILE)
        low[rows, :] = grads[rows, :].astype(jnp.bfloat16)
        return 0

    lax.fori_loop(0, low.shape[0] // TILE, lower, 0)

    def start(slot, _):
        ctx = lax.div(slot, 2)
        y, x, c = lax.div(ctx, 8), lax.rem(lax.div(ctx, 2), 4), lax.rem(ctx, 2)
        place = dkv_hbm.at[c, x * (1 - c) + y * c, y * (1 - c) + x * c]
        pltpu.make_async_copy(
            low.at[pl.ds(slots_ref[slot] * BLK, BLK)],
            place.at[pl.ds(lax.rem(slot, 2) * BLK, BLK)],
            out_sem,
        ).start()
        return 0

    lax.fori_loop(0, 64, start, 0)

    pltpu.make_async_copy(low, low, out_sem).wait()


def attend_forward(slots, mine, queries, gathered):
    smem = pl.BlockSpec(memory_space=pltpu.SMEM)
    vmem = pl.BlockSpec(memory_space=pltpu.VMEM)
    length, width = gathered.shape[0] * BLK, gathered.shape[2]
    return pl.pallas_call(
        forward_kernel,
        out_shape=(
            jax.ShapeDtypeStruct((2, KV_HEADS, HEAD_DIM, LANES), jnp.float32),
            jax.ShapeDtypeStruct((2, KV_HEADS, 1, LANES), jnp.float32),
        ),
        in_specs=[smem, smem, vmem, pl.BlockSpec(memory_space=pl.ANY)],
        out_specs=(vmem, vmem),
        scratch_shapes=[
            pltpu.VMEM((length, width), jnp.bfloat16),
            pltpu.VMEM((KV_HEADS, HEAD_DIM, LANES), jnp.float32),
            pltpu.VMEM((KV_HEADS, 1, LANES), jnp.float32),
            pltpu.VMEM((KV_HEADS, 1, LANES), jnp.float32),
            pltpu.SemaphoreType.DMA,
        ],
        compiler_params=pltpu.CompilerParams(vmem_limit_bytes=48 * 2**20),
        cost_estimate=pl.CostEstimate(
            flops=10_000_000_000, bytes_accessed=8_000_000, transcendentals=5_000_000
        ),
    )(slots, mine, queries, gathered)


def attend_backward(slots, mine, queries, grad_out, out, lse, gathered):
    smem = pl.BlockSpec(memory_space=pltpu.SMEM)
    vmem = pl.BlockSpec(memory_space=pltpu.VMEM)
    hbm = pl.BlockSpec(memory_space=pl.ANY)
    length, width = gathered.shape[0] * BLK, gathered.shape[2]
    return pl.pallas_call(
        backward_kernel,
        out_shape=(
            jax.ShapeDtypeStruct((2, KV_HEADS, HEAD_DIM, LANES), jnp.float32),
            jax.ShapeDtypeStruct((2, 4, 4, 2 * BLK, width), jnp.bfloat16),
        ),
        in_specs=[smem, smem, vmem, vmem, vmem, vmem, hbm],
        out_specs=(vmem, hbm),
        scratch_shapes=[
            pltpu.VMEM((length, width), jnp.bfloat16),
            pltpu.VMEM((length, width), jnp.float32),
            pltpu.VMEM((length, width), jnp.bfloat16),
            pltpu.VMEM((KV_HEADS, 1, LANES), jnp.float32),
            pltpu.VMEM((KV_HEADS, HEAD_DIM, LANES), jnp.float32),
            pltpu.SemaphoreType.DMA,
            pltpu.SemaphoreType.DMA,
        ],
        compiler_params=pltpu.CompilerParams(vmem_limit_bytes=48 * 2**20),
        cost_estimate=pl.CostEstimate(
            flops=20_000_000_000, bytes_accessed=12_000_000, transcendentals=5_000_000
        ),
    )(slots, mine, queries, grad_out, out, lse, gathered)


def by_group(values, before):
    parts = values.reshape(2, BLK, KV_HEADS, GROUP, HEAD_DIM).transpose(0, 2, 3, 1, 4)
    parts = parts.reshape(2, KV_HEADS, GROUP * BLK, HEAD_DIM).astype(jnp.bfloat16)
    return jnp.pad(
        parts,
        ((0, 0), (0, 0), (0, LANES - GROUP * BLK), (before, PAIR - HEAD_DIM - before)),
    )


def from_group(turned):
    parts = turned[..., : GROUP * BLK].reshape(2, KV_HEADS, HEAD_DIM, GROUP, BLK)
    return parts.transpose(0, 4, 1, 3, 2).reshape(2 * BLK, HEADS, HEAD_DIM)


MESH_IDS = pl.DeviceIdType.MESH


def remote(source, target, send_sem, recv_sem, device):
    return pltpu.make_async_remote_copy(
        src_ref=source,
        dst_ref=target,
        send_sem=send_sem,
        recv_sem=recv_sem,
        device_id=device,
        device_id_type=MESH_IDS,
    )


def greet(devices):
    barrier = pltpu.get_barrier_semaphore()
    for device in devices:
        pl.semaphore_signal(barrier, inc=1, device_id=device, device_id_type=MESH_IDS)
    pl.semaphore_wait(barrier, len(devices))


def ffn_kernel(
    h_ref, cot_columns_ref, gate_up_ref, down_ref,
    dh_ref, partial_ref, grads_ref,
    rows, cot_ref, grad, hid, dgate, dup, mine, from_sibling, kept, halves, passed, arrived,
    gather_send, gather_recv, sib_send, sib_recv, ring_send, ring_recv,
):
    x, c = lax.axis_index("x"), lax.axis_index("c")
    right, left, across = lax.rem(x + 1, 4), lax.rem(x + 3, 4), lax.rem(x + 2, 4)
    other = 1 - c
    to_right, to_left, to_sibling = {"x": right}, {"x": left}, {"c": other}
    half = BLK
    top, low = pl.ds(0, half), pl.ds(half, half)
    greet((to_right, to_left, to_sibling))

    rows[x, c] = h_ref[...]
    spot = rows.at[x, c]
    first = [
        remote(spot, spot, gather_send.at[0], gather_recv.at[0], to_right),
        remote(spot, spot, gather_send.at[1], gather_recv.at[1], to_left),
        remote(spot, spot, sib_send.at[0], sib_recv.at[0], to_sibling),
    ]
    for copy in first:
        copy.start()
    from_left, from_right, from_far = rows.at[left, c], rows.at[right, c], rows.at[across, c]
    place = lax.broadcasted_iota(jnp.int32, (2 * BLK, 2 * BLK), 0)
    across_place = lax.broadcasted_iota(jnp.int32, (2 * BLK, 2 * BLK), 1)
    identity = jnp.where(place == across_place, 1.0, 0.0).astype(jnp.bfloat16)
    for chip in range(4):
        for core in range(2):
            turned = multiply_transposed(identity, cot_columns_ref[chip, core])
            cot_ref[chip, core] = turned.astype(jnp.bfloat16)
    gate_w, up_w = gate_up_ref[0], gate_up_ref[1]
    down_w = down_ref[...]

    def work(chip, step):
        block = rows[chip].reshape(4 * BLK, D)
        gate = multiply(block, gate_w)
        up = multiply(block, up_w)
        grad_hidden = multiply_transposed(cot_ref[chip].reshape(4 * BLK, D), down_w)
        sigmoid = 1.0 / (1.0 + jnp.exp(-gate))
        silu = gate * sigmoid
        hidden = (silu * up).astype(jnp.bfloat16)
        grad_gate = (grad_hidden * up * sigmoid * (1.0 + gate * (1.0 - sigmoid))).astype(jnp.bfloat16)
        grad_up = (grad_hidden * silu).astype(jnp.bfloat16)
        hid[chip] = hidden
        dgate[chip] = grad_gate
        dup[chip] = grad_up
        grad_rows = multiply_transposed(grad_gate, gate_w) + multiply_transposed(grad_up, up_w)
        kept[step] = grad_rows.reshape(2, 2 * BLK, D)
        mine[step] = kept[step, other].astype(jnp.bfloat16)
        copy = remote(
            mine.at[step], from_sibling.at[step], sib_send.at[4 + step], sib_recv.at[4 + step], to_sibling
        )
        copy.start()
        partial_ref[chip] = multiply(hidden, down_w).astype(jnp.bfloat16).reshape(2, 2 * BLK, D)
        return copy

    first[2].wait_recv()
    backs = [work(x, 0)]
    first[0].wait_recv()
    forward_right = remote(
        from_left.at[top], from_left.at[top], gather_send.at[2], gather_recv.at[2], to_right
    )
    forward_right.start()
    sib_left = remote(from_left, from_left, sib_send.at[1], sib_recv.at[1], to_sibling)
    sib_left.start()
    first[1].wait_recv()
    forward_left = remote(
        from_right.at[low], from_right.at[low], gather_send.at[3], gather_recv.at[3], to_left
    )
    forward_left.start()
    sib_right = remote(from_right, from_right, sib_send.at[2], sib_recv.at[2], to_sibling)
    sib_right.start()
    sib_left.wait_recv()
    backs.append(work(left, 1))
    sib_right.wait_recv()
    backs.append(work(right, 2))
    forward_right.wait_recv()
    forward_left.wait_recv()
    sib_far = remote(from_far, from_far, sib_send.at[3], sib_recv.at[3], to_sibling)
    sib_far.start()
    sib_far.wait_recv()
    backs.append(work(across, 3))

    backs[3].wait_recv()
    far = kept[3, c] + from_sibling[3].astype(jnp.float32)
    halves[...] = far.astype(jnp.bfloat16)
    far_right = remote(halves.at[top], arrived.at[0, top], ring_send.at[0], ring_recv.at[0], to_right)
    far_left = remote(halves.at[low], arrived.at[0, low], ring_send.at[1], ring_recv.at[1], to_left)
    far_right.start()
    far_left.start()
    unit = FF // 32
    slabs = [(z, y) for z in range(4) for y in range(4)]

    def keep(start, down):
        for z, y in slabs:
            line, column = (z, y) if down else (y, z)
            piece = grad[
                line * unit : (line + 1) * unit, column * (D // 4) : (column + 1) * (D // 4)
            ]
            grads_ref[z, y, start : start + unit] = piece.astype(jnp.bfloat16)

    grad[...] = contract_rows(
        dgate[...].reshape(16 * BLK, FF // 8), rows[...].reshape(16 * BLK, D)
    )
    keep(0, False)
    for step in range(3):
        backs[step].wait_recv()
        kept[step, c] += from_sibling[step].astype(jnp.float32)
    far_right.wait_recv()
    passed[0, top] = (kept[2, c, top] + arrived[0, top].astype(jnp.float32)).astype(jnp.bfloat16)
    passed[0, low] = kept[2, c, low].astype(jnp.bfloat16)
    near_right = remote(passed.at[0], arrived.at[1], ring_send.at[2], ring_recv.at[2], to_right)
    near_right.start()
    far_left.wait_recv()
    passed[1, top] = kept[1, c, top].astype(jnp.bfloat16)
    passed[1, low] = (kept[1, c, low] + arrived[0, low].astype(jnp.float32)).astype(jnp.bfloat16)
    near_left = remote(passed.at[1], arrived.at[2], ring_send.at[3], ring_recv.at[3], to_left)
    near_left.start()
    grad[...] = contract_rows(
        dup[...].reshape(16 * BLK, FF // 8), rows[...].reshape(16 * BLK, D)
    )
    keep(unit, False)
    grad[...] = contract_rows(
        hid[...].reshape(16 * BLK, FF // 8), cot_ref[...].reshape(16 * BLK, D)
    )
    keep(2 * unit, True)
    near_right.wait_recv()
    near_left.wait_recv()
    dh_ref[...] = (
        kept[0, c] + arrived[1].astype(jnp.float32) + arrived[2].astype(jnp.float32)
    )
    for copy in first + [forward_right, forward_left, sib_left, sib_right, sib_far]:
        copy.wait_send()
    for copy in backs + [far_right, far_left, near_right, near_left]:
        copy.wait_send()


def feed_forward(normed, team_cotangent, gate_up, down):
    vmem = pl.BlockSpec(memory_space=pltpu.VMEM)
    width = FF // 8
    return pl.pallas_call(
        ffn_kernel,
        out_shape=(
            jax.ShapeDtypeStruct((2 * BLK, D), jnp.float32),
            jax.ShapeDtypeStruct((4, 2, 2 * BLK, D), jnp.bfloat16),
            jax.ShapeDtypeStruct((4, 4, 3 * FF // 32, D // 4), jnp.bfloat16),
        ),
        in_specs=[vmem] * 4,
        out_specs=(vmem,) * 3,
        scratch_shapes=[
            pltpu.VMEM((4, 2, 2 * BLK, D), jnp.bfloat16),
            pltpu.VMEM((4, 2, 2 * BLK, D), jnp.bfloat16),
            pltpu.VMEM((width, D), jnp.float32),
            pltpu.VMEM((4, 4 * BLK, width), jnp.bfloat16),
            pltpu.VMEM((4, 4 * BLK, width), jnp.bfloat16),
            pltpu.VMEM((4, 4 * BLK, width), jnp.bfloat16),
            pltpu.VMEM((4, 2 * BLK, D), jnp.bfloat16),
            pltpu.VMEM((4, 2 * BLK, D), jnp.bfloat16),
            pltpu.VMEM((4, 2, 2 * BLK, D), jnp.float32),
            pltpu.VMEM((2 * BLK, D), jnp.bfloat16),
            pltpu.VMEM((2, 2 * BLK, D), jnp.bfloat16),
            pltpu.VMEM((3, 2 * BLK, D), jnp.bfloat16),
            pltpu.SemaphoreType.DMA((4,)),
            pltpu.SemaphoreType.DMA((4,)),
            pltpu.SemaphoreType.DMA((8,)),
            pltpu.SemaphoreType.DMA((8,)),
            pltpu.SemaphoreType.DMA((4,)),
            pltpu.SemaphoreType.DMA((4,)),
        ],
        compiler_params=pltpu.CompilerParams(
            collective_id=1, has_side_effects=True, vmem_limit_bytes=56 * 2**20
        ),
        cost_estimate=pl.CostEstimate(
            flops=6_000_000_000, bytes_accessed=12_000_000, transcendentals=400_000
        ),
    )(normed, team_cotangent, gate_up, down)


def ring_of(axis):
    place = lax.axis_index(axis)
    return place, {axis: lax.rem(place + 1, 4)}, {axis: lax.rem(place + 3, 4)}


def plane_rings():
    x, y, c = lax.axis_index("x"), lax.axis_index("y"), lax.axis_index("c")

    def along(step_x, step_y):
        return {"y": lax.rem(y + step_y, 4), "x": lax.rem(x + step_x, 4)}

    first = (x * (1 - c) + y * c, along(1 - c, c), along(3 * (1 - c), 3 * c))
    second = (y * (1 - c) + x * c, along(c, 1 - c), along(3 * c, 3 * (1 - c)))
    return first, second


def cut(rows):
    top = (rows // 2 + 15) // 16 * 16
    return pl.ds(0, top), pl.ds(top, rows - top)


class RingGather:
    def __init__(self, ring, own, spot, parts, send, recv):
        self.place, self.right, self.left = ring
        self.own, self.spot, self.parts, self.send, self.recv = own, spot, parts, send, recv
        self.begun = []

    def _go(self, source, target, index, device):
        copy = remote(source, target, self.send.at[index], self.recv.at[index], device)
        copy.start()
        self.begun.append(copy)
        return copy

    def near(self):
        target = self.spot(self.place)
        self.to_right = self._go(self.own, target, 0, self.right)
        self.to_left = self._go(self.own, target, 1, self.left)

    def from_left(self):
        self.to_right.wait_recv()
        block = self.spot(lax.rem(self.place + 3, 4))
        piece = block.at[self.parts[0]]
        self.on_right = self._go(piece, piece, 2, self.right)
        return block

    def from_right(self):
        self.to_left.wait_recv()
        block = self.spot(lax.rem(self.place + 1, 4))
        piece = block.at[self.parts[1]]
        self.on_left = self._go(piece, piece, 3, self.left)
        return block

    def from_far(self):
        self.on_right.wait_recv()
        self.on_left.wait_recv()
        return self.spot(lax.rem(self.place + 2, 4))

    def drain(self):
        for copy in self.begun:
            copy.wait_send()


class Passing:
    def __init__(self, send, recv):
        self.send, self.recv, self.copies = send, recv, []
        self.device = {"c": 1 - lax.axis_index("c")}

    def go(self, source, target):
        k = len(self.copies)
        copy = remote(source, target, self.send.at[k], self.recv.at[k], self.device)
        copy.start()
        self.copies.append(copy)

    def wait(self):
        for copy in self.copies:
            copy.wait_recv()

    def drain(self):
        for copy in self.copies:
            copy.wait_send()


def first_gather_kernel(
    w_ref, gain_ref, w_out, gain_out,
    w_send, w_recv, gain_send, gain_recv, sib_send, sib_recv, local,
):
    c = lax.axis_index("c")
    z_ring = ring_of("z")
    greet((z_ring[1], z_ring[2], {"c": 1 - c}))
    passing = Passing(sib_send, sib_recv)
    weights = RingGather(
        z_ring, w_ref.at[c], lambda i: w_out.at[c, i], cut(w_ref.shape[1]), w_send, w_recv
    )
    gains = RingGather(
        z_ring, gain_ref, lambda i: gain_out.at[i], cut(gain_ref.shape[0]), gain_send, gain_recv
    )
    weights.near()
    gains.near()
    z = z_ring[0]
    own = [
        pltpu.make_async_copy(w_ref, w_out.at[:, z], local.at[0]),
        pltpu.make_async_copy(gain_ref, gain_out.at[z], local.at[1]),
    ]
    for copy in own:
        copy.start()
    for turn in ("from_left", "from_right", "from_far"):
        block = getattr(weights, turn)()
        passing.go(block, block)
        getattr(gains, turn)()
    passing.wait()
    for copy in own:
        copy.wait()
    weights.drain()
    gains.drain()
    passing.drain()


def second_gather_kernel(
    kv_ref, o_ref, down_ref, kv_out, o_out, down_out,
    kv_send, kv_recv, o_send, o_recv, down_send, down_recv, sib_send, sib_recv, o_sib_send, o_sib_recv, local,
):
    x, y, c = lax.axis_index("x"), lax.axis_index("y"), lax.axis_index("c")
    z_ring = ring_of("z")
    first, second = plane_rings()
    greet((first[1], first[2], second[1], second[2], z_ring[1], z_ring[2], {"c": 1 - c}))
    a0 = first[0]

    def spot(a, b):
        return kv_out.at[b * (1 - c) + a * c, a * (1 - c) + b * c, c]

    rows = cut(kv_ref.shape[0])
    passing = Passing(sib_send, sib_recv)
    o_passing = Passing(o_sib_send, o_sib_recv)

    def hand(block):
        passing.go(block, block)

    stage = RingGather(
        first, kv_ref, lambda a: spot(a, second[0]), rows, kv_send.at[0], kv_recv.at[0]
    )

    def spread_ring(k, shift, own):
        a = lax.rem(a0 + shift, 4)
        ring = RingGather(
            second, own, lambda b: spot(a, b), rows, kv_send.at[1 + k], kv_recv.at[1 + k]
        )
        ring.near()
        return ring

    stage.near()
    ring_own = spread_ring(0, 0, kv_ref)
    passing.go(kv_ref, spot(a0, second[0]))
    z_rings = (
        RingGather(z_ring, o_ref.at[c], lambda i: o_out.at[c, i], cut(o_ref.shape[1]), o_send, o_recv),
        RingGather(z_ring, down_ref, lambda i: down_out.at[i], cut(down_ref.shape[0]), down_send, down_recv),
    )
    for ring in z_rings:
        ring.near()
    z = z_ring[0]
    own = [
        pltpu.make_async_copy(kv_ref, kv_out.at[y, x, c], local.at[0]),
        pltpu.make_async_copy(o_ref, o_out.at[:, z], local.at[1]),
        pltpu.make_async_copy(down_ref, down_out.at[z], local.at[2]),
    ]
    for copy in own:
        copy.start()
    block = stage.from_left()
    ring_left = spread_ring(1, 3, block)
    hand(block)
    block = stage.from_right()
    ring_right = spread_ring(2, 1, block)
    hand(block)
    block = stage.from_far()
    ring_far = spread_ring(3, 2, block)
    hand(block)
    plane = (ring_own, ring_left, ring_right, ring_far)
    for turn in ("from_left", "from_right"):
        for ring in plane:
            hand(getattr(ring, turn)())
        block = getattr(z_rings[0], turn)()
        o_passing.go(block, block)
        getattr(z_rings[1], turn)()
    for ring in plane:
        hand(ring.from_far())
    block = z_rings[0].from_far()
    o_passing.go(block, block)
    z_rings[1].from_far()
    passing.wait()
    o_passing.wait()
    for copy in own:
        copy.wait()
    for ring in (stage,) + plane + z_rings:
        ring.drain()
    passing.drain()
    o_passing.drain()


def dma(*counts):
    return [pltpu.SemaphoreType.DMA(n if isinstance(n, tuple) else (n,)) for n in counts]


def first_gather(weights, gains):
    hbm = pl.BlockSpec(memory_space=pl.ANY)
    return pl.pallas_call(
        first_gather_kernel,
        out_shape=(
            jax.ShapeDtypeStruct((2, 4) + weights.shape[1:], weights.dtype),
            jax.ShapeDtypeStruct((4,) + gains.shape, gains.dtype),
        ),
        in_specs=[hbm] * 2,
        out_specs=(hbm,) * 2,
        scratch_shapes=dma(4, 4, 4, 4, 3, 3, 2),
        compiler_params=pltpu.CompilerParams(collective_id=2, has_side_effects=True),
        cost_estimate=pl.CostEstimate(flops=0, bytes_accessed=60_000_000, transcendentals=0),
    )(weights, gains)


def second_gather(kv, weight, down):
    hbm = pl.BlockSpec(memory_space=pl.ANY)
    return pl.pallas_call(
        second_gather_kernel,
        out_shape=(
            jax.ShapeDtypeStruct((4, 4, 2) + kv.shape, kv.dtype),
            jax.ShapeDtypeStruct((2, 4) + weight.shape[1:], weight.dtype),
            jax.ShapeDtypeStruct((4,) + down.shape, down.dtype),
        ),
        in_specs=[hbm] * 3,
        out_specs=(hbm,) * 3,
        scratch_shapes=dma((5, 4), (5, 4), 4, 4, 4, 4, 16, 16, 3, 3, 3),
        compiler_params=pltpu.CompilerParams(collective_id=3, has_side_effects=True),
        cost_estimate=pl.CostEstimate(flops=0, bytes_accessed=100_000_000, transcendentals=0),
    )(kv, weight, down)


class RingSum:
    def __init__(self, ring, value, parts, far, passed, far_in, near_in, send, recv):
        self.place, self.right, self.left = ring
        self.value, self.parts = value, parts
        self.far, self.passed, self.far_in, self.near_in = far, passed, far_in, near_in
        self.send, self.recv = send, recv
        self.begun = []

    def _go(self, source, target, index, device):
        copy = remote(source, target, self.send.at[index], self.recv.at[index], device)
        copy.start()
        self.begun.append(copy)
        return copy

    def send_far(self):
        top, low = self.parts
        other = lax.rem(self.place + 2, 4)
        for part in self.parts:
            self.far[part] = self.value(other, part).astype(jnp.bfloat16)
        self.far_right = self._go(self.far.at[top], self.far_in.at[top], 0, self.right)
        self.far_left = self._go(self.far.at[low], self.far_in.at[low], 1, self.left)

    def send_right(self):
        top, low = self.parts
        other = lax.rem(self.place + 1, 4)
        self.passed[0, low] = self.value(other, low).astype(jnp.bfloat16)
        self.far_right.wait_recv()
        total = self.value(other, top) + self.far_in[top].astype(jnp.float32)
        self.passed[0, top] = total.astype(jnp.bfloat16)
        self.near_right = self._go(self.passed.at[0], self.near_in.at[0], 2, self.right)

    def send_left(self):
        top, low = self.parts
        other = lax.rem(self.place + 3, 4)
        self.passed[1, top] = self.value(other, top).astype(jnp.bfloat16)
        self.far_left.wait_recv()
        total = self.value(other, low) + self.far_in[low].astype(jnp.float32)
        self.passed[1, low] = total.astype(jnp.bfloat16)
        self.near_left = self._go(self.passed.at[1], self.near_in.at[1], 3, self.left)

    def arrive(self):
        self.near_right.wait_recv()
        self.near_left.wait_recv()

    def total(self, part):
        return (
            self.value(self.place, part)
            + self.near_in[0, part].astype(jnp.float32)
            + self.near_in[1, part].astype(jnp.float32)
        )

    def drain(self):
        for copy in self.begun:
            copy.wait_send()


def ring_scratch(shape):
    return [
        pltpu.VMEM(shape, jnp.bfloat16),
        pltpu.VMEM((2,) + shape, jnp.bfloat16),
        pltpu.VMEM(shape, jnp.bfloat16),
        pltpu.VMEM((2,) + shape, jnp.bfloat16),
        pltpu.SemaphoreType.DMA((4,)),
        pltpu.SemaphoreType.DMA((4,)),
    ]


HALVES = (pl.ds(0, 2), pl.ds(2, 2))


class PlaneSum:
    def __init__(self, rings, parts, theirs, one, two, sib_send, sib_recv):
        self.first, self.second = rings
        self.parts, self.theirs = parts, theirs
        self.c = lax.axis_index("c")
        self.sib_send, self.sib_recv = sib_send, sib_recv
        middle, one, two = one[0], one[1:], two
        self.middle = middle
        shape = middle.shape[1:]
        self.rows = (pl.ds(0, shape[0] // 2), pl.ds(shape[0] // 2, shape[0] // 2))
        self.ring_one = RingSum(self.first, self._both, HALVES, *one)
        self.ring_two = RingSum(self.second, self._middle, self.rows, *two)

    def _both(self, a, part):
        mine = self.parts[self.c, a, part].astype(jnp.float32)
        return mine + self.theirs[a, part].astype(jnp.float32)

    def _middle(self, b, part):
        return self.middle[b, part].astype(jnp.float32)

    def hand(self, k):
        a = lax.rem(self.second[0] + (2, 1, 3, 0)[k], 4)
        copy = remote(
            self.parts.at[1 - self.c, a],
            self.theirs.at[a],
            self.sib_send.at[k],
            self.sib_recv.at[k],
            {"c": 1 - self.c},
        )
        copy.start()
        return copy

    def along_first(self, handed):
        one = self.ring_one
        handed[0].wait_recv()
        one.send_far()
        handed[1].wait_recv()
        one.send_right()
        handed[2].wait_recv()
        one.send_left()
        handed[3].wait_recv()

    def along_second(self):
        one, two = self.ring_one, self.ring_two
        one.arrive()
        for part in HALVES:
            self.middle[part] = one.total(part).astype(jnp.bfloat16)
        two.send_far()
        two.send_right()
        two.send_left()

    def drain(self, handed):
        for copy in handed:
            copy.wait_send()
        self.ring_one.drain()
        self.ring_two.drain()


ORDER = (2, 1, 3, 0)


def fill(plane, left_ref, right_ref):
    c = lax.axis_index("c")
    wide = left_ref.shape[3]

    rows = plane.parts.shape[-1]

    def product(core, a):
        lhs = left_ref[core, a].reshape(4 * wide, left_ref.shape[4])
        block = multiply(lhs, right_ref[...]).astype(jnp.bfloat16)
        for z in range(4):
            piece = block[:, z * LANES : z * LANES + rows]
            plane.parts[core, a, :, z] = piece.reshape(4, wide, rows)

    handed = []
    for k in range(4):
        product(1 - c, lax.rem(plane.second[0] + ORDER[k], 4))
        handed.append(plane.hand(k))
    for k in range(4):
        product(c, lax.rem(plane.first[0] + ORDER[k], 4))
    return handed


def pairs_sum_kernel(parts, ffn, kv_out, ffn_out, theirs, middle, *scratch):
    sems, rest = scratch[:2], scratch[2:]
    one, two, three = (rest[6 * k : 6 * k + 6] for k in range(3))
    first, second = plane_rings()
    z_ring = ring_of("z")
    greet((first[1], first[2], second[1], second[2], z_ring[1], z_ring[2], {"c": 1 - lax.axis_index("c")}))
    pairs = PlaneSum((first, second), parts, theirs, (middle,) + one, two, *sems)
    handed = [pairs.hand(k) for k in range(4)]
    along_z = RingSum(
        z_ring, lambda i, part: ffn[i, part].astype(jnp.float32), HALVES, *three
    )
    along_z.send_far()
    pairs.along_first(handed)
    along_z.send_right()
    along_z.send_left()
    pairs.along_second()
    pairs.ring_two.arrive()
    for part in pairs.rows:
        kv_out[part] = pairs.ring_two.total(part)
    along_z.arrive()
    for part in HALVES:
        ffn_out[part] = along_z.total(part).astype(jnp.bfloat16)
    pairs.drain(handed)
    along_z.drain()


def pairs_sum(parts, ffn):
    vmem = pl.BlockSpec(memory_space=pltpu.VMEM)
    block, share = parts.shape[3:], ffn.shape[2:]
    return pl.pallas_call(
        pairs_sum_kernel,
        out_shape=(
            jax.ShapeDtypeStruct(block, jnp.float32),
            jax.ShapeDtypeStruct((4,) + share, jnp.bfloat16),
        ),
        in_specs=[vmem] * 2,
        out_specs=(vmem,) * 2,
        scratch_shapes=[
            pltpu.VMEM((4, 4) + block, jnp.bfloat16),
            pltpu.VMEM((4,) + block, jnp.bfloat16),
        ]
        + dma(4, 4)
        + ring_scratch((4,) + block)
        + ring_scratch(block)
        + ring_scratch((4,) + share),
        compiler_params=pltpu.CompilerParams(
            collective_id=4, has_side_effects=True, vmem_limit_bytes=56 * 2**20
        ),
    )(parts, ffn)


def weights_sum_kernel(
    left_ref, right_ref, ffn_ref, out_ref, ffn_out, down_out,
    parts, theirs, middle, last, down_own, *scratch,
):
    sems, rest = scratch[:2], scratch[2:]
    one, two, three, four = (rest[6 * k : 6 * k + 6] for k in range(4))
    down_send, down_recv, local = rest[24:]
    x, c = lax.axis_index("x"), lax.axis_index("c")
    first, second = plane_rings()
    z_ring, y_ring = ring_of("z"), ring_of("y")
    team = [
        {"x": lax.rem(x + step, 4), "c": (1 - c) if swap else c}
        for swap in (0, 1)
        for step in range(4)
        if step + swap > 0
    ]
    greet([y_ring[1], y_ring[2], z_ring[1], z_ring[2]] + team)
    along_y = RingSum(
        y_ring,
        lambda i, part: ffn_ref[i, part].astype(jnp.float32),
        cut(ffn_ref.shape[1]),
        *four,
    )
    along_y.send_far()
    plane = PlaneSum((first, second), parts, theirs, (middle,) + one, two, *sems)
    handed = fill(plane, left_ref, right_ref)
    along_y.send_right()
    along_y.send_left()
    plane.along_first(handed)
    along_y.arrive()
    for part in along_y.parts:
        ffn_out[part] = along_y.total(part).astype(jnp.bfloat16)
    third = down_own.shape[0]
    down_own[...] = ffn_out[2 * third : 3 * third]
    own = pltpu.make_async_copy(down_own, down_out.at[x, c], local)
    own.start()
    downs = [
        remote(down_own, down_out.at[x, c], down_send.at[k], down_recv.at[k], device)
        for k, device in enumerate(team)
    ]
    for copy in downs:
        copy.start()
    plane.along_second()
    plane.ring_two.arrive()
    for part in plane.rows:
        last[part] = plane.ring_two.total(part)
    along_z = RingSum(z_ring, lambda i, part: last[i, part], cut(left_ref.shape[3]), *three)
    along_z.send_far()
    along_z.send_right()
    along_z.send_left()
    along_z.arrive()
    for part in along_z.parts:
        out_ref[part] = along_z.total(part)
    own.wait()
    for copy in downs:
        copy.wait_recv()
    plane.drain(handed)
    along_z.drain()
    along_y.drain()
    for copy in downs:
        copy.wait_send()


def weights_sum(left, right, ffn):
    vmem = pl.BlockSpec(memory_space=pltpu.VMEM)
    hbm = pl.BlockSpec(memory_space=pl.ANY)
    block = (left.shape[3], D // 4)
    share = ffn.shape[1:]
    down = (share[0] // 3, share[1])
    return pl.pallas_call(
        weights_sum_kernel,
        out_shape=(
            jax.ShapeDtypeStruct(block, jnp.float32),
            jax.ShapeDtypeStruct(share, jnp.bfloat16),
            jax.ShapeDtypeStruct((4, 2) + down, jnp.bfloat16),
        ),
        in_specs=[vmem] * 3,
        out_specs=(vmem, vmem, hbm),
        scratch_shapes=[
            pltpu.VMEM((2, 4, 4, 4) + block, jnp.bfloat16),
            pltpu.VMEM((4, 4, 4) + block, jnp.bfloat16),
            pltpu.VMEM((4, 4) + block, jnp.bfloat16),
            pltpu.VMEM((4,) + block, jnp.float32),
            pltpu.VMEM(down, jnp.bfloat16),
        ]
        + dma(4, 4)
        + ring_scratch((4, 4) + block)
        + ring_scratch((4,) + block)
        + ring_scratch(block)
        + ring_scratch(share)
        + dma(7, 7)
        + [pltpu.SemaphoreType.DMA],
        compiler_params=pltpu.CompilerParams(
            collective_id=5, has_side_effects=True, vmem_limit_bytes=60 * 2**20
        ),
    )(left, right, ffn)


def shards(
    tokens, cotangent, slot_blocks, norm_gains,
    w_query, w_key, w_value, w_output, w_gate, w_up, w_down,
):
    inputs = tokens[0].astype(jnp.float32)
    row_count = inputs.shape[0]
    ctx_index = lax.axis_index(CTX)
    member = lax.axis_index(TEAM)
    mine = lax.dynamic_slice_in_dim(slot_blocks, 2 * ctx_index, 2)
    offsets = jnp.arange(BLK, dtype=jnp.int32)
    local_pos = (mine[:, None] * BLK + offsets[None, :]).reshape(row_count)
    cosine, sine = rope_tables(local_pos)

    kv_parts = [
        w[:, h * HEAD_DIM : (h + 1) * HEAD_DIM] for h in range(KV_HEADS) for w in (w_key, w_value)
    ]
    w_kv = jnp.concatenate(kv_parts, axis=1)
    wide = w_kv.shape[1] // 2
    gain_rows = jnp.pad(norm_gains, (0, 32 * 128 - norm_gains.shape[0])).reshape(32, 128)
    full_kv, gains = first_gather(jnp.stack([w_kv[:, :wide], w_kv[:, wide:]]), gain_rows)
    full_kv = full_kv.reshape(2, D, wide)
    gains = gains.reshape(4, -1)[:, : D // 2].reshape(2 * D).astype(jnp.float32)

    source = jnp.arange(FF // 8, dtype=jnp.int32)
    source = source // (FF // 32) * (FF // 4) + member * (FF // 32) + source % (FF // 32)
    picked = (jnp.arange(FF, dtype=jnp.int32)[:, None] == source[None, :]).astype(jnp.bfloat16)
    my_gate_up = jnp.stack(
        [multiply(w_gate, picked).astype(jnp.bfloat16), multiply(w_up, picked).astype(jnp.bfloat16)]
    )
    my_down = lax.dynamic_slice_in_dim(w_down, member * (FF // 32), FF // 32)
    upstream_low = cotangent[0]
    gate_up = lax.all_gather(my_gate_up, "z", axis=1, tiled=True)
    full_output = lax.all_gather(w_output, "z", axis=0, tiled=True)
    team_upstream = lax.all_gather(cotangent, TEAM, axis=0, tiled=True)
    my_query = jnp.stack([w_query[:, : D // 2], w_query[:, D // 2 :]])
    gain_first, gain_second = gains[:D], gains[D:]

    root_first = lax.rsqrt(jnp.mean(inputs * inputs, axis=-1, keepdims=True) + epsilon)
    normed_first = (inputs * root_first * gain_first).astype(jnp.bfloat16)
    raw_kv = jnp.concatenate(
        [multiply(normed_first, full_kv[0]), multiply(normed_first, full_kv[1])], axis=1
    )
    pairs = raw_kv.reshape(row_count, KV_HEADS, 2, HEAD_DIM)
    keys = rotate(pairs[:, :, 0], cosine, sine)
    packed = jnp.stack([keys, pairs[:, :, 1]], axis=2).astype(jnp.bfloat16)
    packed = packed.reshape(row_count, KV_HEADS * PAIR)
    gathered, full_query, down = second_gather(packed, my_query, my_down)
    down = down.reshape(FF // 8, D)
    gathered = gathered.reshape(64, BLK, KV_HEADS * PAIR)
    full_query = full_query.reshape(2, D, D // 2)
    raw = jnp.concatenate(
        [multiply(normed_first, full_query[0]), multiply(normed_first, full_query[1])], axis=1
    )
    queries = rotate(raw.reshape(row_count, HEADS, HEAD_DIM), cosine, sine)
    query_rows = by_group(queries.astype(jnp.bfloat16) * jnp.bfloat16(0.125), 0)
    out_turned, lse = attend_forward(slot_blocks, mine, query_rows, gathered)
    attended = from_group(out_turned).reshape(row_count, D).astype(jnp.bfloat16)
    middle = inputs + multiply(attended, full_output)

    root_second = lax.rsqrt(jnp.mean(middle * middle, axis=-1, keepdims=True) + epsilon)
    normed_second = (middle * root_second * gain_second).astype(jnp.bfloat16)
    grad_normed_second, partial, grad_ffn = feed_forward(
        normed_second,
        team_upstream.swapaxes(1, 2).reshape(4, 2, D, row_count),
        gate_up,
        down,
    )
    down_sum = lax.psum_scatter(
        partial.reshape(8, row_count, D), TEAM, scatter_dimension=0, tiled=True
    )

    norm_part, gain_grad_second = norm_backward(
        grad_normed_second, middle, root_second, gain_second
    )
    grad_middle = upstream_low.astype(jnp.float32) + norm_part
    middle_low = grad_middle.astype(jnp.bfloat16)

    grad_attended = multiply_transposed(middle_low, full_output).astype(jnp.bfloat16)

    grad_rows = by_group(grad_attended.reshape(row_count, HEADS, HEAD_DIM), HEAD_DIM)
    query_turned, grad_pairs = attend_backward(
        slot_blocks, mine, query_rows, grad_rows, out_turned, lse, gathered
    )
    grad_query_raw = rotate(from_group(query_turned), cosine, -sine)
    grad_query_raw = grad_query_raw.reshape(row_count, D).astype(jnp.bfloat16)

    def by_owner(columns):
        columns = columns.reshape((4, 4, 2) + columns.shape[1:])
        return jnp.stack([columns[:, :, 0].swapaxes(0, 1), columns[:, :, 1]])

    def by_rows(values):
        parts = values.reshape(-1, 4, D // 4)
        return jnp.pad(parts, ((0, 0), (0, 0), (0, LANES - D // 4))).reshape(-1, 4 * LANES)

    own_pairs, part_ffn = pairs_sum(grad_pairs, grad_ffn)
    own_pairs = own_pairs.reshape(row_count, KV_HEADS, 2, HEAD_DIM)
    grad_key_raw = rotate(own_pairs[:, :, 0], cosine, -sine)
    grad_kv = jnp.stack([grad_key_raw, own_pairs[:, :, 1]], axis=2)
    grad_kv = grad_kv.reshape(row_count, -1).astype(jnp.bfloat16)
    grad_normed_first = multiply_transposed(grad_query_raw[:, : D // 2], full_query[0])
    grad_normed_first += multiply_transposed(grad_query_raw[:, D // 2 :], full_query[1])
    grad_normed_first += multiply_transposed(grad_kv[:, :wide], full_kv[0])
    grad_normed_first += multiply_transposed(grad_kv[:, wide:], full_kv[1])
    norm_first_part, gain_grad_first = norm_backward(
        grad_normed_first, inputs, root_first, gain_first
    )
    input_grad = grad_middle + norm_first_part

    kv_columns = grad_kv.reshape(row_count, KV_HEADS, 2, HEAD_DIM)
    k_columns = kv_columns[:, :, 0].reshape(row_count, 32, 10)
    v_columns = kv_columns[:, :, 1].reshape(row_count, 32, 10)
    q_columns = grad_query_raw.reshape(row_count, 32, 30)
    above = jnp.concatenate([q_columns, k_columns, v_columns], axis=2)
    above = jnp.pad(above, ((0, 0), (0, 0), (0, 46)))
    below = jnp.pad(middle_low.reshape(row_count, 32, 30), ((0, 0), (0, 0), (50, 16)))
    columns = jnp.concatenate([above, below], axis=0).transpose(1, 2, 0)
    owners = jnp.arange(32, dtype=jnp.int32)
    spots = jnp.arange(96, dtype=jnp.int32)
    mark = (owners[:, None, None] == owners[None, None, :]) & (spots[None, :, None] == 80)
    columns = jnp.concatenate([columns, mark.astype(jnp.bfloat16)], axis=2)
    gain_rows = jnp.concatenate([gain_grad_first, gain_grad_second]).astype(jnp.bfloat16)
    gain_rows = jnp.pad(gain_rows.reshape(32, 4, 15), ((0, 0), (0, 0), (0, LANES - 15)))
    gain_rows = gain_rows.reshape(32, 4 * LANES)
    rows = jnp.concatenate([by_rows(normed_first), by_rows(attended), gain_rows], axis=0)
    sums, sum_ffn, team_down = weights_sum(by_owner(columns), rows, part_ffn)
    down_sum, sums = lax.optimization_barrier((down_sum, sums))
    layer_out = (middle + down_sum[0].astype(jnp.float32)).astype(jnp.bfloat16)[None]
    sums = sums.T
    ffn_columns = sum_ffn[:160].T.astype(jnp.float32)
    sum_down = lax.dynamic_slice_in_dim(
        team_down.reshape(FF // 4, D // 4), member * 30, 30, axis=1
    ).astype(jnp.float32)
    return (
        layer_out,
        input_grad[None],
        sums[:15, 80],
        sums[:, :30],
        sums[:, 30:40],
        sums[:, 40:50],
        sums[:, 50:80],
        ffn_columns[:, :80],
        ffn_columns[:, 80:],
        sum_down,
    )


def solution(mesh):
    fine = Mesh(mesh.devices.reshape(4, 4, 2, 4), ALL)
    weight = P("z", None)
    return jax.shard_map(
        shards,
        mesh=fine,
        in_specs=(
            P("z", CTX, None),
            P("z", CTX, None),
            P(),
            P("z"),
        )
        + (weight,) * 7,
        out_specs=(
            P("z", CTX, None),
            P("z", CTX, None),
            P(ALL),
        )
        + (P("z", CTX),) * 7,
        check_vma=False,
    )
```
